512 devices in a mesh: dp: 2 (over y_lo), storage: 32 (over y_hi, z), feature: 8 (over x, core).
Axes of the slice: x: 4, y: 8 (y_hi: 4, y_lo: 2; y = y_hi * 2 + y_lo), z: 8, core: 2. Of those that a mesh axis runs over, the one named last changes fastest.
Arguments:
- activations: bfloat16 [8192, 4096], P(('dp', 'storage'), 'feature'), may hold values from -6 to 6
- expert_ids: int32 [8192, 1], P(('dp', 'storage')), may hold values from 0 to 1; in each aligned block of 128 rows (0 to 127, 128 to 255, ...) at most 96 rows name the same one
- pre_bias: float32 [2, 4096], P('dp', 'feature'), may hold values from -3 to 3
- enc_weight: bfloat16 [2, 4096, 4096], P('dp', 'feature', 'storage'), may hold values from -0.09375 to 0.09375
- enc_bias: float32 [2, 4096], P('dp'), may hold values from -3 to 3
- dec_weight: bfloat16 [2, 4096, 4096], P('dp', 'feature', 'storage'), may hold values from -0.09375 to 0.09375
Outputs:
- rebuilt: bfloat16 [8192, 4096], P(('dp', 'storage'), 'feature')
- row_error: float32 [8192], P(('dp', 'storage'))
The draws below stay inside these ranges and needn't reach their ends.
Inputs may be any that keep to these rules, and one draw needn't show every extreme that they name: `expert_ids`: each row names one expert. Among the rows of one index of dp and storage, at most 96 name the same expert, and that bound is reached.
All inputs are finite; a program needn't handle non-finite values.
Results may differ from the reference program's by a relative error of at most 0.018.
Values may be sent and summed in bfloat16 or wider, within the bound.
A program may use at most 64 MiB of HBM per device.

```python
import math
import jax
import jax.numpy as jnp
import numpy as np
from jax import lax

D = 4096
LAT = 4096
EXPERTS = 2
ROWS_DEV = 128
CAP = 96
ROWS = 8192
N_FEATURE = 8


def block_scale(rng, shape, shards, smallest, high):
    def one(dim, blocks):
        heights = jax.random.uniform(jax.random.fold_in(jax.random.fold_in(rng, 6), dim), (blocks,), jnp.float32, smallest / len(shards), high / len(shards))
        return jnp.repeat(jnp.exp(heights), shape[dim] // blocks).reshape((-1,) + (1,) * (len(shape) - dim - 1))

    level = one(*shards[0])
    for cut in shards[1:]:
        level = level * one(*cut)
    return level


def assign_block(own_key, own, number, rows, count, top, reach, slope):
    ranking = jax.random.permutation(own_key, count)
    heavy_load, ordinary = shares(count, rows * top, reach, slope, True), shares(count, rows * top, reach, slope, False)
    places = jnp.arange(count)

    def named(tallies, turn):
        used = int((tallies > 0).sum())
        fixed = max(1, used // 4)
        passed = fixed + (places - fixed + turn * (used - fixed)) % max(1, count - fixed)
        return jnp.zeros((count,), jnp.int32).at[ranking[jnp.where(places < fixed, places, passed)]].set(jnp.asarray(tallies, jnp.int32))

    tallies = jnp.where(number % 4 == 0, named(heavy_load, number // 4), named(ordinary, number - number // 4 - 1))
    mixed = jax.random.permutation(jax.random.fold_in(own, 3), count)
    source_of, sink = mixed[0:count // 2 * 2:2], mixed[1:count // 2 * 2:2]
    room = jnp.minimum(tallies[source_of] - 1, reach - tallies[sink]) // 2
    room = jnp.where((source_of == ranking[0]) | (sink == ranking[0]) | (tallies[sink] == 0), 0, jnp.maximum(room, 0))
    passed = jax.random.randint(jax.random.fold_in(own, 4), (count // 2,), 0, 1 << 20) % (room + 1)
    tallies = tallies.at[source_of].add(-passed).at[sink].add(passed)
    members = jnp.searchsorted(jnp.cumsum(tallies), jnp.arange(rows * top), side="right").astype(jnp.int32)
    grid = members.reshape(top, rows).T
    grid = grid[jax.random.permutation(jax.random.fold_in(own, 1), rows)]
    turn = jax.random.randint(jax.random.fold_in(own, 2), (rows, 1), 0, top)
    return jnp.take_along_axis(grid, (jnp.arange(top)[None, :] + turn) % top, axis=1)


def shares(count, total, limit, skew, full):
    loads = [(1 << 20) // math.isqrt(standing ** skew) + 1 for standing in range(1, count + 1)]
    largest = limit if full else min(limit, max(-(-total // count), total * loads[0] // sum(loads)))
    least = 1 if total - largest >= count - 1 else 0
    given, spare = [largest] + [least] * (count - 1), total - largest - least * (count - 1)
    while spare > 0:
        free = [i for i in range(1, count) if given[i] < largest] or [i for i in range(1, count) if given[i] < limit]
        whole, budget = sum([loads[i] for i in free]), spare
        for i in free:
            more = min(limit - given[i], max(1, budget * loads[i] // whole), spare)
            given[i] = given[i] + more
            spare = spare - more
    return np.array(given)


def bell_draw(rng, shape, scale, limit, cuts=(), kind=jnp.bfloat16):
    result = scale * jax.random.normal(rng, shape, jnp.float32)
    if cuts:
        result = result * block_scale(rng, shape, cuts, -0.22, 0.18)
    return jnp.clip(result, -limit, limit).astype(kind)


def setup_inputs(seed: int = 0) -> dict:
    streams_of = jax.random.split(jax.random.key(seed), 7)
    activations = bell_draw(streams_of[0], (ROWS, D), 1.0, 6.0, ((0, 64), (1, 8)))
    expert_ids_keys = jax.random.split(jax.random.fold_in(streams_of[1], 1), ROWS // ROWS_DEV)
    expert_ids_turns = jax.random.permutation(jax.random.fold_in(streams_of[1], 3), ROWS // ROWS_DEV)
    expert_ids = jax.vmap(lambda own, number: assign_block(jax.random.fold_in(streams_of[1], 2), own, number, ROWS_DEV, EXPERTS, 1, CAP, 2))(expert_ids_keys, expert_ids_turns).reshape((ROWS, 1))
    pre_bias = bell_draw(streams_of[2], (EXPERTS, D), 0.5, 3.0, ((0, 2), (1, 8)), jnp.float32)
    enc_weight = bell_draw(streams_of[3], (EXPERTS, D, LAT), D ** -0.5, 0.09375, ((0, 2), (1, 8), (2, 32)))
    enc_bias = bell_draw(streams_of[4], (EXPERTS, LAT), 0.5, 3.0, ((0, 2),), jnp.float32)
    dec_weight = bell_draw(streams_of[5], (EXPERTS, D, LAT), LAT ** -0.5, 0.09375, ((0, 2), (1, 8), (2, 32)))
    return dict(activations=activations, expert_ids=expert_ids, pre_bias=pre_bias, enc_weight=enc_weight, enc_bias=enc_bias, dec_weight=dec_weight)


def reference(activations, expert_ids, pre_bias, enc_weight, enc_bias, dec_weight):
    row_count = activations.shape[0]
    feat_width = activations.shape[1]
    lat_width = enc_weight.shape[2]
    experts = enc_weight.shape[0]
    expert_of = expert_ids[:, 0].astype(jnp.int32)
    onehot = (expert_of[:, None] == jnp.arange(experts, dtype=jnp.int32)[None, :]).astype(jnp.int32)
    counts = jnp.sum(onehot, 0)
    padded = (counts + 127) // 128 * 128
    block_ends = jnp.cumsum(padded).astype(jnp.int32)
    block_starts = block_ends - padded
    rank_in = jnp.sum((jnp.cumsum(onehot, 0) - onehot) * onehot, 1)
    slot_of = (jnp.sum(block_starts[None, :] * onehot, 1) + rank_in).astype(jnp.int32)
    blocks = row_count // 128 + experts
    buffer = jnp.zeros((blocks * 128, feat_width), jnp.bfloat16).at[slot_of].set(activations)
    firsts = jnp.arange(blocks, dtype=jnp.int32) * 128
    owners = jnp.minimum(jnp.sum((firsts[:, None] >= block_ends[None, :]).astype(jnp.int32), 1), experts - 1).astype(jnp.int32)

    def one_block(packed):
        block_rows, owner_id = packed
        bias_pre = lax.dynamic_index_in_dim(pre_bias, owner_id, 0, keepdims=False)
        enc_mat = lax.dynamic_index_in_dim(enc_weight, owner_id, 0, keepdims=False)
        dec_mat = lax.dynamic_index_in_dim(dec_weight, owner_id, 0, keepdims=False)
        bias_enc = lax.dynamic_index_in_dim(enc_bias, owner_id, 0, keepdims=False)
        centred = (block_rows.astype(jnp.float32) - bias_pre[None, :]).astype(jnp.bfloat16)
        partials = jnp.einsum("rgd,gdl->grl",
                              centred.reshape(128, N_FEATURE, -1).astype(jnp.float32),
                              enc_mat.reshape(N_FEATURE, -1, lat_width).astype(jnp.float32))
        rounded = lax.optimization_barrier(partials.astype(jnp.bfloat16)).astype(jnp.float32)
        latents = jax.nn.relu(jnp.sum(rounded, 0) + bias_enc[None, :]).astype(jnp.bfloat16)
        decoded = lax.dot_general(latents, dec_mat, (((1,), (1,)), ((), ())), preferred_element_type=jnp.float32)
        return (decoded + bias_pre[None, :]).astype(jnp.bfloat16)

    results = lax.map(one_block, (buffer.reshape(blocks, 128, feat_width), owners))
    rebuilt = results.reshape(blocks * 128, feat_width)[slot_of]
    diff = rebuilt.astype(jnp.float32) - activations.astype(jnp.float32)
    row_error = jnp.mean(diff * diff, axis=1)
    return rebuilt, row_error
```

```python
import functools

import jax
import jax.numpy as jnp
from jax import lax
from jax.experimental import pallas as pl
from jax.experimental.pallas import tpu as pltpu
from jax.sharding import PartitionSpec as P

MESH = pl.DeviceIdType.MESH
D = 4096
N = 8
NX = 4
ROWS = 128
FEAT = 512
BLK = 128
LATS = 512
CH = 2
F32 = jnp.float32
BF16 = jnp.bfloat16


def ring_steps(direction, chunk):
    far = chunk < CH // 2 if direction == 0 else chunk >= CH // 2
    return 4 if far else 3


def kernel(
    act, ids, pre_bias, enc_w, enc_b, dec_w, out, err,
    a_buf, w_buf, d_buf, meta, ids_all, mask, pair_out, pair_in, x_out, x_in, own_sum, lat, dec, acc_out, acc_in,
    err_all,
    a_ss, a_rs, w_ss, w_rs, d_ss, d_rs, m_ss, m_rs, i_ss, i_rs, p_ss, p_rs, x_ss, x_rs, g_ss, g_rs, s_ss, s_rs,
    o_ss, o_rs, e_ss, e_rs,
):
    dp = lax.axis_index("dp")
    storage = lax.axis_index("storage")
    feature = lax.axis_index("feature")
    z = storage % 8
    y = (storage // 8) * 2 + dp
    x = feature // 2
    c = feature % 2

    def at(yy, zz, ff):
        return (yy % 2, (yy // 2) * 8 + zz, ff)

    def z_at(off):
        return at(y, (z + off + N) % N, feature)

    def y_at(off):
        return at((y + off + N) % N, z, feature)

    def f_at(xx, cc):
        return at(y, z, xx * 2 + cc)

    def w_slot(yy):
        return (yy % 2) * 4 + yy // 2

    pending = []

    def send(src, dst, ss, rs, dev):
        cp = pltpu.make_async_remote_copy(
            src_ref=src, dst_ref=dst, send_sem=ss, recv_sem=rs, device_id=dev, device_id_type=MESH
        )
        cp.start()
        pending.append(cp)

    def arrive(dst, ss, rs):
        pltpu.make_async_remote_copy(
            src_ref=dst, dst_ref=dst, send_sem=ss, recv_sem=rs, device_id=f_at(x, 1 - c), device_id_type=MESH
        ).wait_recv()

    barrier = pltpu.get_barrier_semaphore()
    greet = [z_at(k) for k in range(1, N)] + [y_at(1), y_at(-1)]
    greet += [at(y, z, (feature + k) % 8) for k in range(1, 8)]
    for dev in greet:
        pl.semaphore_signal(barrier, inc=1, device_id=dev, device_id_type=MESH)

    a_buf[z] = act[...]
    w_buf[w_slot(y)] = enc_w[0]
    d_buf[w_slot(y)] = dec_w[0].astype(F32).T.astype(BF16)
    meta[dp, 0:1, :] = pre_bias[...]
    for q in range(4):
        meta[dp, 1:2, q * BLK:(q + 1) * BLK] = enc_b[0:1, pl.ds(pl.multiple_of((q * 8 + z) * BLK, BLK), BLK)]
    ids_all[z] = jnp.broadcast_to(ids[...], (8, ROWS))

    pl.semaphore_wait(barrier, len(greet))

    send(meta.at[dp], meta.at[dp], m_ss, m_rs, at(y + 1 - 2 * dp, z, feature))

    def ring_piece(buf, slot_of, coord, direction, step, chunk):
        sign = 1 if direction == 0 else -1
        block = slot_of((coord - step * sign + N) % N)
        size = buf.shape[1] // CH
        return buf.at[block, pl.ds(chunk * size, size)]

    def ring_send(buf, slot_of, coord, to, ss, rs, direction, step, chunk):
        ref = ring_piece(buf, slot_of, coord, direction, step, chunk)
        sign = 1 if direction == 0 else -1
        send(ref, ref, ss.at[direction, step, chunk], rs.at[direction, step, chunk], to(sign))

    def ring_arrive(buf, slot_of, coord, ss, rs, direction, step, chunk):
        ref = ring_piece(buf, slot_of, coord, direction, step + 1, chunk)
        arrive(ref, ss.at[direction, step, chunk], rs.at[direction, step, chunk])

    a_ring = (a_buf, lambda b: b, z, z_at, a_ss, a_rs)
    w_ring = (w_buf, w_slot, y, y_at, w_ss, w_rs)
    d_ring = (d_buf, w_slot, y, y_at, d_ss, d_rs)

    def gather_step(rings, step):
        for chunk in range(CH):
            for buf, slot_of, coord, to, ss, rs in rings:
                for direction in range(2):
                    steps = ring_steps(direction, chunk)
                    if 1 <= step <= steps:
                        ring_arrive(buf, slot_of, coord, ss, rs, direction, step - 1, chunk)
                    if step < steps:
                        ring_send(buf, slot_of, coord, to, ss, rs, direction, step, chunk)

    gather_step((a_ring, w_ring), 0)
    for k in range(1, N):
        send(ids_all.at[z], ids_all.at[z], i_ss.at[k], i_rs.at[k], z_at(k))

    def mask_of(b):
        mask[b] = jnp.broadcast_to(ids_all[b, 0:1, :].astype(F32), (ROWS, ROWS)).T

    mask_of(z)
    for k in range(1, N):
        src = (z - k + N) % N
        arrive(ids_all.at[src], i_ss.at[k], i_rs.at[k])
        mask_of(src)
    arrive(meta.at[1 - dp], m_ss, m_rs)

    for step in range(1, 5):
        gather_step((a_ring, w_ring), step)

    gather_step((d_ring,), 0)

    def wide(b):
        tile = mask[b]
        return jnp.concatenate([tile] * 4, axis=1) > 0.5

    enc = [jnp.concatenate([w_buf[e * 4 + q] for q in range(4)], axis=1) for e in range(2)]

    def encode(blocks):
        left, right = [], []
        for b in blocks:
            second = wide(b)
            rows = a_buf[b].astype(F32)
            left.append(jnp.where(second, 0.0, rows - meta[0, 0:1, :]).astype(BF16))
            right.append(jnp.where(second, rows - meta[1, 0:1, :], 0.0).astype(BF16))
        return jnp.dot(jnp.concatenate(left, 0), enc[0], preferred_element_type=F32) + jnp.dot(
            jnp.concatenate(right, 0), enc[1], preferred_element_type=F32
        )

    sibling = f_at(x, 1 - c)
    offsets = (2, 1, 3, 0)
    for pair in (offsets[:2], offsets[2:]):
        sums = encode([2 * ((x + o) % NX) + 1 - c for o in pair])
        for j, o in enumerate(pair):
            pair_out[o] = sums[j * ROWS:(j + 1) * ROWS].astype(BF16)
            send(pair_out.at[o], pair_in.at[o], p_ss.at[o], p_rs.at[o], sibling)
    for pair in (offsets[:2], offsets[2:]):
        sums = encode([2 * ((x + o) % NX) + c for o in pair])
        for j, o in enumerate(pair):
            arrive(pair_in.at[o], p_ss.at[o], p_rs.at[o])
            total = sums[j * ROWS:(j + 1) * ROWS] + pair_in[o].astype(F32)
            if o == 0:
                own_sum[...] = total
            else:
                x_out[o] = total.astype(BF16)
                send(x_out.at[o], x_in.at[o], x_ss.at[o], x_rs.at[o], f_at((x + o) % NX, c))

    gather_step((d_ring,), 1)

    for o in range(1, NX):
        arrive(x_in.at[o], x_ss.at[o], x_rs.at[o])
    pre = own_sum[...] + (x_in[1].astype(F32) + x_in[2].astype(F32) + x_in[3].astype(F32))
    pre += jnp.where(wide(feature), meta[1, 1:2, :], meta[0, 1:2, :])
    lat[feature] = jnp.maximum(pre, 0.0).astype(BF16)
    for o in (2, 1, 3):
        send(lat.at[feature], lat.at[feature], g_ss.at[o], g_rs.at[o], f_at((x + o) % NX, c))
    send(lat.at[feature], lat.at[feature], s_ss.at[0], s_rs.at[0], sibling)

    gather_step((d_ring,), 2)
    for o in (1, 3, 2):
        src = 2 * ((x - o + NX) % NX) + c
        arrive(lat.at[src], g_ss.at[o], g_rs.at[o])
        send(lat.at[src], lat.at[src], s_ss.at[o], s_rs.at[o], sibling)
    gather_step((d_ring,), 3)
    gather_step((d_ring,), 4)
    for o in range(NX):
        src = 2 * ((x - o + NX) % NX) + 1 - c
        arrive(lat.at[src], s_ss.at[o], s_rs.at[o])

    weights = d_buf[...].reshape(N * BLK, FEAT)

    def decode(blocks):
        rows = []
        for b in blocks:
            second = wide(b)
            value = lat[b].astype(F32)
            rows.append(
                jnp.concatenate(
                    [jnp.where(second, 0.0, value).astype(BF16), jnp.where(second, value, 0.0).astype(BF16)], axis=1
                )
            )
        return jnp.dot(jnp.concatenate(rows, 0), weights, preferred_element_type=F32)

    half = ROWS // 2

    def hop(direction, step, h, value):
        acc_out[direction, step, h] = value.astype(BF16)
        send(
            acc_out.at[direction, step, h], acc_in.at[direction, step, h],
            o_ss.at[direction, step, h], o_rs.at[direction, step, h], z_at(1 if direction == 0 else -1),
        )

    def landed(direction, step, h):
        arrive(acc_in.at[direction, step, h], o_ss.at[direction, step, h], o_rs.at[direction, step, h])
        return acc_in[direction, step, h].astype(F32)

    part = decode([(z + 4) % N])
    hop(0, 0, 0, part[:half])
    hop(1, 0, 1, part[half:])
    for step in range(1, 4):
        far = 4 - step
        dec[...] = decode([(z + far) % N, (z - far + N) % N])
        for direction in range(2):
            for h in (direction, 1 - direction):
                value = dec[direction * ROWS + h * half:direction * ROWS + (h + 1) * half, :]
                if step > 1 or h == direction:
                    value = value + landed(direction, step - 1, h)
                hop(direction, step, h, value)
    dec[0:ROWS] = decode([z])
    squares = []
    for h in range(2):
        span = slice(h * half, (h + 1) * half)
        total = dec[span, :] + (landed(0, 3, h) + landed(1, 3, h))
        second = jnp.concatenate([mask[z, span, :]] * 4, axis=1) > 0.5
        total += jnp.where(second, meta[1, 0:1, :], meta[0, 0:1, :])
        rebuilt = total.astype(BF16)
        out[span, :] = rebuilt
        diff = rebuilt.astype(F32) - act[span, :].astype(F32)
        square = diff * diff
        squares.append(square[:, 0:128] + square[:, 128:256] + square[:, 256:384] + square[:, 384:512])
    mine = jnp.sum(jnp.concatenate(squares, 0).T, axis=0, keepdims=True)
    err_all[0] = jnp.broadcast_to(mine, (8, ROWS))
    for k in range(1, 8):
        send(err_all.at[0], err_all.at[k], e_ss.at[k], e_rs.at[k], at(y, z, (feature + k) % 8))
    total = mine
    for k in range(1, 8):
        arrive(err_all.at[k], e_ss.at[k], e_rs.at[k])
        total += err_all[k, 0:1, :]
    err[...] = total * (1.0 / D)
    for cp in pending:
        cp.wait_send()


def local(activations, expert_ids, pre_bias, enc_weight, enc_bias, dec_weight):
    vmem = pl.BlockSpec(memory_space=pltpu.VMEM)
    dma = pltpu.SemaphoreType.DMA
    rebuilt, row_error = pl.pallas_call(
        kernel,
        out_shape=(
            jax.ShapeDtypeStruct((ROWS, FEAT), BF16),
            jax.ShapeDtypeStruct((1, ROWS), F32),
        ),
        in_specs=[vmem] * 6,
        out_specs=(vmem, vmem),
        scratch_shapes=[
            pltpu.VMEM((N, ROWS, FEAT), BF16),
            pltpu.VMEM((N, FEAT, BLK), BF16),
            pltpu.VMEM((N, BLK, FEAT), BF16),
            pltpu.VMEM((2, 8, FEAT), F32),
            pltpu.VMEM((N, 8, ROWS), jnp.int32),
            pltpu.VMEM((N, ROWS, ROWS), F32),
            pltpu.VMEM((NX, ROWS, LATS), BF16),
            pltpu.VMEM((NX, ROWS, LATS), BF16),
            pltpu.VMEM((NX, ROWS, LATS), BF16),
            pltpu.VMEM((NX, ROWS, LATS), BF16),
            pltpu.VMEM((ROWS, LATS), F32),
            pltpu.VMEM((N, ROWS, LATS), BF16),
            pltpu.VMEM((2 * ROWS, FEAT), F32),
            pltpu.VMEM((2, 4, 2, ROWS // 2, FEAT), BF16),
            pltpu.VMEM((2, 4, 2, ROWS // 2, FEAT), BF16),
            pltpu.VMEM((N, 8, ROWS), F32),
            dma((2, 4, CH)), dma((2, 4, CH)),
            dma((2, 4, CH)), dma((2, 4, CH)),
            dma((2, 4, CH)), dma((2, 4, CH)),
            dma, dma,
            dma((N,)), dma((N,)),
            dma((NX,)), dma((NX,)),
            dma((NX,)), dma((NX,)),
            dma((NX,)), dma((NX,)),
            dma((NX,)), dma((NX,)),
            dma((2, 4, 2)), dma((2, 4, 2)),
            dma((N,)), dma((N,)),
        ],
        compiler_params=pltpu.CompilerParams(
            collective_id=0, has_side_effects=True, vmem_limit_bytes=48 * 2**20
        ),
    )(activations, expert_ids.reshape(1, ROWS), pre_bias, enc_weight, enc_bias, dec_weight)
    return rebuilt, row_error.reshape(ROWS)


def solution(mesh):
    return jax.shard_map(
        local,
        mesh=mesh,
        in_specs=(
            P(("dp", "storage"), "feature"),
            P(("dp", "storage"), None),
            P("dp", "feature"),
            P("dp", "feature", "storage"),
            P("dp", None),
            P("dp", "feature", "storage"),
        ),
        out_specs=(P(("dp", "storage"), "feature"), P(("dp", "storage"))),
        check_vma=False,
    )
```

```python
import functools

import jax
import jax.numpy as jnp
from jax import lax
from jax.experimental import pallas as pl
from jax.experimental.pallas import tpu as pltpu
from jax.sharding import PartitionSpec as P

MESH = pl.DeviceIdType.MESH
D = 4096
N = 8
NX = 4
ROWS = 128
FEAT = 512
BLK = 128
LATS = 512
GATHER = 4
DCH = 2
K = 4
SUB = ROWS // K
F32 = jnp.float32
BF16 = jnp.bfloat16


def ring_steps(direction, chunk, chunks):
    far = chunk < chunks // 2 if direction == 0 else chunk >= chunks // 2
    return 4 if far else 3


def kernel(
    act, ids, pre_bias, enc_w, enc_b, dec_w, out, err,
    a_buf, w_buf, w_cat, d_raw, d_buf, pb_raw, eb_raw, ids_raw, meta, ids_all, mask,
    pair_own, pair_out, pair_in, x_own, x_out, x_in, lat, dec, acc_out, acc_in, square, err_all,
    l_sem, a_ss, a_rs, w_ss, w_rs, d_ss, d_rs, m_ss, m_rs, i_ss, i_rs, p_ss, p_rs, x_ss, x_rs, g_ss, g_rs, s_ss, s_rs,
    o_ss, o_rs, e_ss, e_rs,
):
    dp = lax.axis_index("dp")
    storage = lax.axis_index("storage")
    feature = lax.axis_index("feature")
    z = storage % 8
    y = (storage // 8) * 2 + dp
    x = feature // 2
    c = feature % 2

    def at(yy, zz, ff):
        return (yy % 2, (yy // 2) * 8 + zz, ff)

    def z_at(off):
        return at(y, (z + off + N) % N, feature)

    def y_at(off):
        return at((y + off + N) % N, z, feature)

    def f_at(xx, cc):
        return at(y, z, xx * 2 + cc)

    def w_slot(yy):
        return (yy % 2) * 4 + yy // 2

    sibling = f_at(x, 1 - c)
    pending = []

    def send(src, dst, ss, rs, dev):
        cp = pltpu.make_async_remote_copy(
            src_ref=src, dst_ref=dst, send_sem=ss, recv_sem=rs, device_id=dev, device_id_type=MESH
        )
        cp.start()
        pending.append(cp)

    def arrive(dst, ss, rs):
        pltpu.make_async_remote_copy(
            src_ref=dst, dst_ref=dst, send_sem=ss, recv_sem=rs, device_id=sibling, device_id_type=MESH
        ).wait_recv()

    barrier = pltpu.get_barrier_semaphore()
    greet = [z_at(k) for k in range(1, N)] + [y_at(1), y_at(-1)]
    greet += [at(y, z, (feature + k) % 8) for k in range(1, 8)]
    for dev in greet:
        pl.semaphore_signal(barrier, inc=1, device_id=dev, device_id_type=MESH)

    loads = [
        pltpu.make_async_copy(src, dst, l_sem.at[j])
        for j, (src, dst) in enumerate(
            (
                (dec_w.at[0], d_raw),
                (act, a_buf.at[z]),
                (enc_w.at[0], w_buf.at[w_slot(y)]),
                (ids, ids_raw),
                (pre_bias, pb_raw),
                (enc_b, eb_raw),
            )
        )
    ]
    for cp in loads:
        cp.start()
    for cp in loads:
        cp.wait()
    d_buf[w_slot(y)] = d_raw[...].astype(F32).T.astype(BF16)
    meta[dp, 0:1, :] = pb_raw[...]
    for q in range(4):
        meta[dp, 1:2, q * BLK:(q + 1) * BLK] = eb_raw[0:1, pl.ds(pl.multiple_of((q * 8 + z) * BLK, BLK), BLK)]
    ids_all[z] = jnp.broadcast_to(ids_raw[...], (8, ROWS))

    pl.semaphore_wait(barrier, len(greet))

    def ring_piece(buf, slot_of, coord, chunks, direction, step, chunk):
        sign = 1 if direction == 0 else -1
        block = slot_of((coord - step * sign + N) % N)
        size = buf.shape[1] // chunks
        return buf.at[block, pl.ds(chunk * size, size)]

    def ring_send(buf, slot_of, coord, chunks, to, ss, rs, direction, step, chunk):
        ref = ring_piece(buf, slot_of, coord, chunks, direction, step, chunk)
        sign = 1 if direction == 0 else -1
        send(ref, ref, ss.at[direction, step, chunk], rs.at[direction, step, chunk], to(sign))

    def ring_arrive(buf, slot_of, coord, chunks, ss, rs, direction, step, chunk):
        ref = ring_piece(buf, slot_of, coord, chunks, direction, step + 1, chunk)
        arrive(ref, ss.at[direction, step, chunk], rs.at[direction, step, chunk])

    a_ring = (a_buf, lambda b: b, z, GATHER, z_at, a_ss, a_rs)
    w_ring = (w_buf, w_slot, y, GATHER, y_at, w_ss, w_rs)
    d_ring = (d_buf, w_slot, y, DCH, y_at, d_ss, d_rs)

    def gather_step(rings, step):
        for chunk in range(rings[0][3]):
            for buf, slot_of, coord, chunks, to, ss, rs in rings:
                for direction in range(2):
                    steps = ring_steps(direction, chunk, chunks)
                    if 1 <= step <= steps:
                        ring_arrive(buf, slot_of, coord, chunks, ss, rs, direction, step - 1, chunk)
                    if step < steps:
                        ring_send(buf, slot_of, coord, chunks, to, ss, rs, direction, step, chunk)

    def spread(yy):
        lanes = pl.ds(pl.multiple_of((yy // 2) * BLK, BLK), BLK)
        w_cat[yy % 2, :, lanes] = w_buf[w_slot(yy)]

    gather_step((a_ring, w_ring), 0)
    send(meta.at[dp], meta.at[dp], m_ss, m_rs, at(y + 1 - 2 * dp, z, feature))
    for k in range(1, N):
        send(ids_all.at[z], ids_all.at[z], i_ss.at[k], i_rs.at[k], z_at(k))

    def mask_of(b):
        mask[b] = jnp.broadcast_to(ids_all[b, 0:1, :].astype(F32), (ROWS, ROWS)).T

    mask_of(z)
    spread(y)
    gather_step((a_ring, w_ring), 1)
    for k in range(1, N):
        src = (z - k + N) % N
        arrive(ids_all.at[src], i_ss.at[k], i_rs.at[k])
        mask_of(src)
    arrive(meta.at[1 - dp], m_ss, m_rs)
    for step in range(2, 5):
        spread((y + step - 1) % N)
        spread((y - step + 1 + N) % N)
        gather_step((a_ring, w_ring), step)
        if step == 3:
            gather_step((d_ring,), 0)
    spread((y + 4) % N)

    def wide(b, k):
        return jnp.concatenate([mask[b, k * SUB:(k + 1) * SUB, :]] * 4, axis=1) > 0.5

    offsets = (2, 1, 3, 0)

    def encode(k):
        left, right = [], []
        for b in [2 * ((x + o) % NX) + 1 - c for o in offsets] + [2 * ((x + o) % NX) + c for o in offsets]:
            second = wide(b, k)
            rows = a_buf[b, k * SUB:(k + 1) * SUB, :].astype(F32)
            left.append(jnp.where(second, 0.0, rows - meta[0, 0:1, :]).astype(BF16))
            right.append(jnp.where(second, rows - meta[1, 0:1, :], 0.0).astype(BF16))
        sums = jnp.dot(jnp.concatenate(left, 0), w_cat[0], preferred_element_type=F32) + jnp.dot(
            jnp.concatenate(right, 0), w_cat[1], preferred_element_type=F32
        )
        pair_out[k] = sums[:NX * SUB].astype(BF16)
        send(pair_out.at[k], pair_in.at[k], p_ss.at[k], p_rs.at[k], sibling)
        pair_own[k] = sums[NX * SUB:]

    def pair_sum(k):
        arrive(pair_in.at[k], p_ss.at[k], p_rs.at[k])
        total = pair_own[k] + pair_in[k].astype(F32)
        x_own[k] = total[3 * SUB:]
        x_out[k] = total[:3 * SUB].astype(BF16).reshape(3, SUB, LATS)
        for j in range(3):
            send(x_out.at[k, j], x_in.at[k, j], x_ss.at[k, j], x_rs.at[k, j], f_at((x + offsets[j]) % NX, c))

    def activate(k):
        for j in range(3):
            arrive(x_in.at[k, j], x_ss.at[k, j], x_rs.at[k, j])
        pre = x_own[k] + (x_in[k, 0].astype(F32) + x_in[k, 1].astype(F32) + x_in[k, 2].astype(F32))
        pre += jnp.where(wide(feature, k), meta[1, 1:2, :], meta[0, 1:2, :])
        lat[k, c, x] = jnp.maximum(pre, 0.0).astype(BF16)
        mine = lat.at[k, c, x]
        for j in range(3):
            send(mine, mine, g_ss.at[k, j], g_rs.at[k, j], f_at((x + offsets[j]) % NX, c))

    def share(k):
        for j in (1, 2, 0):
            got = lat.at[k, c, (x - offsets[j] + NX) % NX]
            arrive(got, g_ss.at[k, j], g_rs.at[k, j])
        send(lat.at[k, c], lat.at[k, c], s_ss.at[k], s_rs.at[k], sibling)

    def z_far(direction, k):
        return 4 if k % 2 == direction else 3

    def hop(direction, step, k, value):
        acc_out[direction, step, k] = value.astype(BF16)
        send(
            acc_out.at[direction, step, k], acc_in.at[direction, step, k],
            o_ss.at[direction, step, k], o_rs.at[direction, step, k], z_at(1 if direction == 0 else -1),
        )

    def landed(direction, step, k):
        arrive(acc_in.at[direction, step, k], o_ss.at[direction, step, k], o_rs.at[direction, step, k])
        return acc_in[direction, step, k].astype(F32)

    targets = (4, 3, -3, 2, -2, 1, -1, 0)

    def decode(k):
        arrive(lat.at[k, 1 - c], s_ss.at[k], s_rs.at[k])
        rows = []
        for t in targets:
            b = (z + t + N) % N
            second = wide(b, k)
            value = lat[k, b % 2, b // 2].astype(F32)
            rows.append(
                jnp.concatenate(
                    [jnp.where(second, 0.0, value).astype(BF16), jnp.where(second, value, 0.0).astype(BF16)], axis=1
                )
            )
        dec[k] = jnp.dot(
            jnp.concatenate(rows, 0), d_buf[...].reshape(N * BLK, FEAT), preferred_element_type=F32
        ).reshape(N, SUB, FEAT)
        hop(k % 2, 0, k, dec[k, 0])

    def z_step(k, step):
        for direction in (k % 2, 1 - k % 2):
            value = dec[k, 2 * step - 1 + direction]
            if step > 1 or z_far(direction, k) == 4:
                value = value + landed(direction, step - 1, k)
            hop(direction, step, k, value)

    def finish(k):
        span = slice(k * SUB, (k + 1) * SUB)
        total = dec[k, 7] + (landed(k % 2, 3, k) + landed(1 - k % 2, 3, k))
        total += jnp.where(wide(z, k), meta[1, 0:1, :], meta[0, 0:1, :])
        rebuilt = total.astype(BF16)
        out[span, :] = rebuilt
        diff = rebuilt.astype(F32) - a_buf[z, span, :].astype(F32)
        sq = diff * diff
        square[span, :] = sq[:, 0:128] + sq[:, 128:256] + sq[:, 256:384] + sq[:, 384:512]

    encode(0)
    encode(1)
    pair_sum(0)
    encode(2)
    pair_sum(1)
    encode(3)
    pair_sum(2)
    pair_sum(3)
    gather_step((d_ring,), 1)
    activate(0)
    gather_step((d_ring,), 2)
    activate(1)
    activate(2)
    gather_step((d_ring,), 3)
    activate(3)
    share(0)
    gather_step((d_ring,), 4)
    share(1)
    decode(0)
    share(2)
    decode(1)
    z_step(0, 1)
    share(3)
    decode(2)
    z_step(1, 1)
    decode(3)
    z_step(0, 2)
    z_step(2, 1)
    z_step(1, 2)
    z_step(3, 1)
    z_step(0, 3)
    z_step(2, 2)
    z_step(1, 3)
    z_step(3, 2)
    finish(0)
    z_step(2, 3)
    finish(1)
    z_step(3, 3)
    finish(2)
    finish(3)

    mine = jnp.sum(square[...].T, axis=0, keepdims=True)
    err_all[0] = jnp.broadcast_to(mine, (8, ROWS))
    for k in range(1, 8):
        send(err_all.at[0], err_all.at[k], e_ss.at[k], e_rs.at[k], at(y, z, (feature + k) % 8))
    total = mine
    for k in range(1, 8):
        arrive(err_all.at[k], e_ss.at[k], e_rs.at[k])
        total += err_all[k, 0:1, :]
    err[...] = total * (1.0 / D)
    for cp in pending:
        cp.wait_send()


def local(activations, expert_ids, pre_bias, enc_weight, enc_bias, dec_weight):
    vmem = pl.BlockSpec(memory_space=pltpu.VMEM)
    dma = pltpu.SemaphoreType.DMA
    rebuilt, row_error = pl.pallas_call(
        kernel,
        out_shape=(
            jax.ShapeDtypeStruct((ROWS, FEAT), BF16),
            jax.ShapeDtypeStruct((1, ROWS), F32),
        ),
        in_specs=[pl.BlockSpec(memory_space=pltpu.HBM)] * 6,
        out_specs=(vmem, vmem),
        scratch_shapes=[
            pltpu.VMEM((N, ROWS, FEAT), BF16),
            pltpu.VMEM((N, FEAT, BLK), BF16),
            pltpu.VMEM((2, FEAT, LATS), BF16),
            pltpu.VMEM((FEAT, BLK), BF16),
            pltpu.VMEM((N, BLK, FEAT), BF16),
            pltpu.VMEM((1, FEAT), F32),
            pltpu.VMEM((1, D), F32),
            pltpu.VMEM((1, ROWS), jnp.int32),
            pltpu.VMEM((2, 8, FEAT), F32),
            pltpu.VMEM((N, 8, ROWS), jnp.int32),
            pltpu.VMEM((N, ROWS, ROWS), F32),
            pltpu.VMEM((K, NX * SUB, LATS), F32),
            pltpu.VMEM((K, NX * SUB, LATS), BF16),
            pltpu.VMEM((K, NX * SUB, LATS), BF16),
            pltpu.VMEM((K, SUB, LATS), F32),
            pltpu.VMEM((K, 3, SUB, LATS), BF16),
            pltpu.VMEM((K, 3, SUB, LATS), BF16),
            pltpu.VMEM((K, 2, NX, SUB, LATS), BF16),
            pltpu.VMEM((K, N, SUB, FEAT), F32),
            pltpu.VMEM((2, 4, K, SUB, FEAT), BF16),
            pltpu.VMEM((2, 4, K, SUB, FEAT), BF16),
            pltpu.VMEM((ROWS, 128), F32),
            pltpu.VMEM((N, 8, ROWS), F32),
            dma((6,)),
            dma((2, 4, GATHER)), dma((2, 4, GATHER)),
            dma((2, 4, GATHER)), dma((2, 4, GATHER)),
            dma((2, 4, DCH)), dma((2, 4, DCH)),
            dma, dma,
            dma((N,)), dma((N,)),
            dma((K,)), dma((K,)),
            dma((K, 3)), dma((K, 3)),
            dma((K, 3)), dma((K, 3)),
            dma((K,)), dma((K,)),
            dma((2, 4, K)), dma((2, 4, K)),
            dma((N,)), dma((N,)),
        ],
        compiler_params=pltpu.CompilerParams(
            collective_id=0, has_side_effects=True, vmem_limit_bytes=64 * 2**20
        ),
    )(activations, expert_ids.reshape(1, ROWS), pre_bias, enc_weight, enc_bias, dec_weight)
    return rebuilt, row_error.reshape(ROWS)


def solution(mesh):
    return jax.shard_map(
        local,
        mesh=mesh,
        in_specs=(
            P(("dp", "storage"), "feature"),
            P(("dp", "storage"), None),
            P("dp", "feature"),
            P("dp", "feature", "storage"),
            P("dp", None),
            P("dp", "feature", "storage"),
        ),
        out_specs=(P(("dp", "storage"), "feature"), P(("dp", "storage"))),
        check_vma=False,
    )
```

```python
import functools

import jax
import jax.numpy as jnp
from jax import lax
from jax.experimental import pallas as pl
from jax.experimental.pallas import tpu as pltpu
from jax.sharding import PartitionSpec as P

MESH = pl.DeviceIdType.MESH
D = 4096
N = 8
NX = 4
ROWS = 128
FEAT = 512
BLK = 128
LATS = 512
GATHER = 4
PARTS = ((4,), (3, -3), (2, -2), (1, -1, 0))
K = len(PARTS)
STRIPE = 16
MOST = STRIPE * max(len(p) for p in PARTS)
ZCH = 4
CHUNK = ROWS // ZCH
F32 = jnp.float32
BF16 = jnp.bfloat16


def ring_steps(direction, chunk, chunks):
    far = chunk < chunks // 2 if direction == 0 else chunk >= chunks // 2
    return 4 if far else 3


def kernel(
    act, ids, pre_bias, enc_w, enc_b, dec_w, out, err,
    a_buf, w_buf, w_cat, d_raw, d_buf, pb_raw, eb_raw, ids_raw, meta, ids_all, mask,
    pair_own, pair_out, pair_in, x_own, x_out, x_in, lat, dec, acc_out, acc_in, square, err_all,
    l_sem, a_ss, a_rs, w_ss, w_rs, d_ss, d_rs, m_ss, m_rs, i_ss, i_rs, p_ss, p_rs, x_ss, x_rs, g_ss, g_rs, s_ss, s_rs,
    o_ss, o_rs, e_ss, e_rs,
):
    dp = lax.axis_index("dp")
    storage = lax.axis_index("storage")
    feature = lax.axis_index("feature")
    z = storage % 8
    y = (storage // 8) * 2 + dp
    x = feature // 2
    c = feature % 2

    def at(yy, zz, ff):
        return (yy % 2, (yy // 2) * 8 + zz, ff)

    def z_at(off):
        return at(y, (z + off + N) % N, feature)

    def y_at(off):
        return at((y + off + N) % N, z, feature)

    def f_at(xx, cc):
        return at(y, z, xx * 2 + cc)

    def w_slot(yy):
        return (yy % 2) * 4 + yy // 2

    sibling = f_at(x, 1 - c)
    pending = []

    def send(src, dst, ss, rs, dev):
        cp = pltpu.make_async_remote_copy(
            src_ref=src, dst_ref=dst, send_sem=ss, recv_sem=rs, device_id=dev, device_id_type=MESH
        )
        cp.start()
        pending.append(cp)

    def arrive(dst, ss, rs):
        pltpu.make_async_remote_copy(
            src_ref=dst, dst_ref=dst, send_sem=ss, recv_sem=rs, device_id=sibling, device_id_type=MESH
        ).wait_recv()

    barrier = pltpu.get_barrier_semaphore()
    greet = [z_at(k) for k in range(1, N)] + [y_at(1), y_at(-1)]
    greet += [at(y, z, (feature + k) % 8) for k in range(1, 8)]
    for dev in greet:
        pl.semaphore_signal(barrier, inc=1, device_id=dev, device_id_type=MESH)

    loads = [
        pltpu.make_async_copy(src, dst, l_sem.at[j])
        for j, (src, dst) in enumerate(
            (
                (dec_w.at[0], d_raw),
                (act, a_buf.at[z]),
                (enc_w.at[0], w_buf.at[w_slot(y)]),
                (ids, ids_raw),
                (pre_bias, pb_raw),
                (enc_b, eb_raw),
            )
        )
    ]
    for cp in loads:
        cp.start()
    for cp in loads:
        cp.wait()
    d_buf[w_slot(y)] = d_raw[...].astype(F32).T.astype(BF16)
    meta[dp, 0:1, :] = pb_raw[...]
    for q in range(4):
        meta[dp, 1:2, q * BLK:(q + 1) * BLK] = eb_raw[0:1, pl.ds(pl.multiple_of((q * 8 + z) * BLK, BLK), BLK)]
    ids_all[z] = jnp.broadcast_to(ids_raw[...], (8, ROWS))

    pl.semaphore_wait(barrier, len(greet))

    def ring_piece(buf, slot_of, coord, chunks, direction, step, chunk):
        sign = 1 if direction == 0 else -1
        block = slot_of((coord - step * sign + N) % N)
        size = buf.shape[1] // chunks
        return buf.at[block, pl.ds(chunk * size, size)]

    def ring_send(buf, slot_of, coord, chunks, to, ss, rs, direction, step, chunk):
        ref = ring_piece(buf, slot_of, coord, chunks, direction, step, chunk)
        sign = 1 if direction == 0 else -1
        send(ref, ref, ss.at[direction, step, chunk], rs.at[direction, step, chunk], to(sign))

    def ring_arrive(buf, slot_of, coord, chunks, ss, rs, direction, step, chunk):
        ref = ring_piece(buf, slot_of, coord, chunks, direction, step + 1, chunk)
        arrive(ref, ss.at[direction, step, chunk], rs.at[direction, step, chunk])

    a_ring = (a_buf, lambda b: b, z, GATHER, z_at, a_ss, a_rs)
    w_ring = (w_buf, w_slot, y, GATHER, y_at, w_ss, w_rs)
    def gather_step(rings, step):
        for chunk in range(GATHER):
            for buf, slot_of, coord, chunks, to, ss, rs in rings:
                for direction in range(2):
                    steps = ring_steps(direction, chunk, chunks)
                    if 1 <= step <= steps:
                        ring_arrive(buf, slot_of, coord, chunks, ss, rs, direction, step - 1, chunk)
                    if step < steps:
                        ring_send(buf, slot_of, coord, chunks, to, ss, rs, direction, step, chunk)

    def spread(yy):
        lanes = pl.ds(pl.multiple_of((yy // 2) * BLK, BLK), BLK)
        w_cat[yy % 2, :, lanes] = w_buf[w_slot(yy)]

    def d_piece(direction, hop, piece):
        size = BLK // 4 if hop == 0 else BLK // 2
        block = w_slot((y - hop * (1 - 2 * direction) + N) % N)
        return d_buf.at[block, pl.ds(piece * size, size)], d_ss.at[direction, hop, piece], d_rs.at[direction, hop, piece]

    def d_send(hop, piece):
        for direction in range(2):
            if hop < 3 or piece == direction:
                ref, ss, rs = d_piece(direction, hop, piece)
                send(ref, ref, ss, rs, y_at(1 - 2 * direction))

    def d_arrive(hop, piece):
        for direction in range(2):
            if hop < 3 or piece == direction:
                ref, ss, rs = d_piece(direction, hop, piece)
                size = ref.shape[0]
                block = w_slot((y - (hop + 1) * (1 - 2 * direction) + N) % N)
                arrive(d_buf.at[block, pl.ds(piece * size, size)], ss, rs)

    gather_step((a_ring, w_ring), 0)
    send(meta.at[dp], meta.at[dp], m_ss, m_rs, at(y + 1 - 2 * dp, z, feature))
    for k in range(1, N):
        send(ids_all.at[z], ids_all.at[z], i_ss.at[k], i_rs.at[k], z_at(k))
    d_send(0, 0)

    def mask_of(b):
        mask[b] = jnp.broadcast_to(ids_all[b, 0:1, :].astype(F32), (ROWS, ROWS)).T

    mask_of(z)
    spread(y)
    gather_step((a_ring, w_ring), 1)
    d_send(0, 1)
    for k in range(1, N):
        src = (z - k + N) % N
        arrive(ids_all.at[src], i_ss.at[k], i_rs.at[k])
        mask_of(src)
    arrive(meta.at[1 - dp], m_ss, m_rs)
    gather_step((a_ring, w_ring), 2)
    d_send(0, 2)
    d_send(0, 3)
    spread((y + 1) % N)
    spread((y + 7) % N)
    gather_step((a_ring, w_ring), 3)
    spread((y + 2) % N)
    spread((y + 6) % N)
    for piece in range(4):
        d_arrive(0, piece)
    d_send(1, 0)
    d_send(1, 1)
    spread((y + 3) % N)
    spread((y + 5) % N)
    gather_step((a_ring, w_ring), 4)
    spread((y + 4) % N)

    def wide(tile):
        return jnp.concatenate([tile] * 4, axis=1) > 0.5

    def stripe(f):
        return pl.ds(pl.multiple_of(f * STRIPE, STRIPE), STRIPE)

    offsets = (2, 1, 3, 0)

    def blocks_of(k):
        return [(z + t + N) % N for t in PARTS[k]]

    def encode(k):
        left, right = [], []
        for f in [2 * ((x + o) % NX) + 1 - c for o in offsets] + [2 * ((x + o) % NX) + c for o in offsets]:
            for b in blocks_of(k):
                second = wide(mask[b, stripe(f), :])
                rows = a_buf[b, stripe(f), :].astype(F32)
                left.append(jnp.where(second, 0.0, rows - meta[0, 0:1, :]).astype(BF16))
                right.append(jnp.where(second, rows - meta[1, 0:1, :], 0.0).astype(BF16))
        sums = jnp.dot(jnp.concatenate(left, 0), w_cat[0], preferred_element_type=F32) + jnp.dot(
            jnp.concatenate(right, 0), w_cat[1], preferred_element_type=F32
        )
        half = NX * STRIPE * len(PARTS[k])
        pair_out[k, :half] = sums[:half].astype(BF16)
        send(pair_out.at[k, pl.ds(0, half)], pair_in.at[k, pl.ds(0, half)], p_ss.at[k], p_rs.at[k], sibling)
        pair_own[k, :half] = sums[half:]

    def pair_sum(k):
        each = STRIPE * len(PARTS[k])
        got = pair_in.at[k, pl.ds(0, NX * each)]
        arrive(got, p_ss.at[k], p_rs.at[k])
        total = pair_own[k, :NX * each] + got[...].astype(F32)
        x_own[k, :each] = total[3 * each:]
        for j in range(3):
            x_out[k, j, :each] = total[j * each:(j + 1) * each].astype(BF16)
            send(
                x_out.at[k, j, pl.ds(0, each)], x_in.at[k, j, pl.ds(0, each)], x_ss.at[k, j], x_rs.at[k, j],
                f_at((x + offsets[j]) % NX, c),
            )

    def lat_of(k, xx):
        each = STRIPE * len(PARTS[k])
        return lat.at[k, c, pl.ds(pl.multiple_of(xx * each, STRIPE), each)]

    def activate(k):
        each = STRIPE * len(PARTS[k])
        pre = x_own[k, :each]
        for j in range(3):
            arrive(x_in.at[k, j, pl.ds(0, each)], x_ss.at[k, j], x_rs.at[k, j])
            pre = pre + x_in[k, j, :each].astype(F32)
        second = jnp.concatenate([wide(mask[b, stripe(feature), :]) for b in blocks_of(k)], 0)
        pre += jnp.where(second, meta[1, 1:2, :], meta[0, 1:2, :])
        mine = lat_of(k, x)
        mine[...] = jnp.maximum(pre, 0.0).astype(BF16)
        for j in range(3):
            send(mine, mine, g_ss.at[k, j], g_rs.at[k, j], f_at((x + offsets[j]) % NX, c))

    def share(k):
        for j in (1, 2, 0):
            arrive(lat_of(k, (x - offsets[j] + NX) % NX), g_ss.at[k, j], g_rs.at[k, j])
        whole = lat.at[k, c, pl.ds(0, NX * STRIPE * len(PARTS[k]))]
        send(whole, whole, s_ss.at[k], s_rs.at[k], sibling)

    def decode(k):
        each = STRIPE * len(PARTS[k])
        arrive(lat.at[k, 1 - c, pl.ds(0, NX * each)], s_ss.at[k], s_rs.at[k])
        left, right = [], []
        for i, b in enumerate(blocks_of(k)):
            second = wide(mask[b])
            starts = [(f % 2, (f // 2) * each + i * STRIPE) for f in range(8)]
            value = jnp.concatenate([lat[k, core, start:start + STRIPE, :] for core, start in starts], 0).astype(F32)
            left.append(jnp.where(second, 0.0, value).astype(BF16))
            right.append(jnp.where(second, value, 0.0).astype(BF16))
        rows = jnp.concatenate([jnp.concatenate(left, 0), jnp.concatenate(right, 0)], axis=1)
        sums = jnp.dot(rows, d_buf[...].reshape(N * BLK, FEAT), preferred_element_type=F32)
        first = sum(len(p) for p in PARTS[:k])
        for i in range(len(PARTS[k])):
            dec[first + i] = sums[i * ROWS:(i + 1) * ROWS]

    def hop(direction, step, h, value):
        acc_out[direction, step, h] = value.astype(BF16)
        send(
            acc_out.at[direction, step, h], acc_in.at[direction, step, h],
            o_ss.at[direction, step, h], o_rs.at[direction, step, h], z_at(1 - 2 * direction),
        )

    def landed(direction, step, h):
        arrive(acc_in.at[direction, step, h], o_ss.at[direction, step, h], o_rs.at[direction, step, h])
        return acc_in[direction, step, h].astype(F32)

    def far(direction, h):
        return h // (ZCH // 2) == direction

    def z_start():
        for i in range(ZCH // 2):
            for direction in range(2):
                h = direction * (ZCH // 2) + i
                hop(direction, 0, h, dec[0, h * CHUNK:(h + 1) * CHUNK])

    def z_step(step):
        for i in range(ZCH):
            for direction in range(2):
                h = (i + (1 - direction) * (ZCH // 2)) % ZCH
                value = dec[2 * step - 1 + direction, h * CHUNK:(h + 1) * CHUNK]
                if step > 1 or far(direction, h):
                    value = value + landed(direction, step - 1, h)
                hop(direction, step, h, value)

    def finish(h):
        span = slice(h * CHUNK, (h + 1) * CHUNK)
        total = dec[7, span] + (landed(0, 3, h) + landed(1, 3, h))
        total += jnp.where(wide(mask[z, span, :]), meta[1, 0:1, :], meta[0, 0:1, :])
        rebuilt = total.astype(BF16)
        out[span, :] = rebuilt
        diff = rebuilt.astype(F32) - a_buf[z, span, :].astype(F32)
        sq = diff * diff
        square[span, :] = sq[:, 0:128] + sq[:, 128:256] + sq[:, 256:384] + sq[:, 384:512]

    def settle(count):
        for cp in pending[:count]:
            cp.wait_send()
        del pending[:count]

    gathered = len(pending)
    encode(0)
    encode(1)
    pair_sum(0)
    pair_sum(1)
    d_arrive(1, 0)
    d_send(2, 0)
    encode(2)
    encode(3)
    d_arrive(1, 1)
    d_send(2, 1)
    activate(0)
    pair_sum(2)
    settle(gathered // 2)
    activate(1)
    pair_sum(3)
    d_arrive(2, 0)
    d_arrive(2, 1)
    d_send(3, 0)
    d_send(3, 1)
    share(0)
    settle(gathered - gathered // 2)
    activate(2)
    d_arrive(3, 0)
    d_arrive(3, 1)
    decode(0)
    z_start()
    share(1)
    activate(3)
    decode(1)
    z_step(1)
    share(2)
    decode(2)
    z_step(2)
    share(3)
    decode(3)
    settle(len(pending) - 6 * ZCH)
    z_step(3)
    settle(len(pending) - 2 * ZCH)
    for h in (0, 2, 1, 3):
        finish(h)

    mine = jnp.sum(square[...].T, axis=0, keepdims=True)
    err_all[0] = jnp.broadcast_to(mine, (8, ROWS))
    for k in range(1, 8):
        send(err_all.at[0], err_all.at[k], e_ss.at[k], e_rs.at[k], at(y, z, (feature + k) % 8))
    total = mine
    for k in range(1, 8):
        arrive(err_all.at[k], e_ss.at[k], e_rs.at[k])
        total += err_all[k, 0:1, :]
    err[...] = total * (1.0 / D)
    settle(len(pending))


def local(activations, expert_ids, pre_bias, enc_weight, enc_bias, dec_weight):
    vmem = pl.BlockSpec(memory_space=pltpu.VMEM)
    dma = pltpu.SemaphoreType.DMA
    rebuilt, row_error = pl.pallas_call(
        kernel,
        out_shape=(
            jax.ShapeDtypeStruct((ROWS, FEAT), BF16),
            jax.ShapeDtypeStruct((1, ROWS), F32),
        ),
        in_specs=[pl.BlockSpec(memory_space=pltpu.HBM)] * 6,
        out_specs=(vmem, vmem),
        scratch_shapes=[
            pltpu.VMEM((N, ROWS, FEAT), BF16),
            pltpu.VMEM((N, FEAT, BLK), BF16),
            pltpu.VMEM((2, FEAT, LATS), BF16),
            pltpu.VMEM((FEAT, BLK), BF16),
            pltpu.VMEM((N, BLK, FEAT), BF16),
            pltpu.VMEM((1, FEAT), F32),
            pltpu.VMEM((1, D), F32),
            pltpu.VMEM((1, ROWS), jnp.int32),
            pltpu.VMEM((2, 8, FEAT), F32),
            pltpu.VMEM((N, 8, ROWS), jnp.int32),
            pltpu.VMEM((N, ROWS, ROWS), F32),
            pltpu.VMEM((K, NX * MOST, LATS), F32),
            pltpu.VMEM((K, NX * MOST, LATS), BF16),
            pltpu.VMEM((K, NX * MOST, LATS), BF16),
            pltpu.VMEM((K, MOST, LATS), F32),
            pltpu.VMEM((K, 3, MOST, LATS), BF16),
            pltpu.VMEM((K, 3, MOST, LATS), BF16),
            pltpu.VMEM((K, 2, NX * MOST, LATS), BF16),
            pltpu.VMEM((N, ROWS, FEAT), F32),
            pltpu.VMEM((2, 4, ZCH, CHUNK, FEAT), BF16),
            pltpu.VMEM((2, 4, ZCH, CHUNK, FEAT), BF16),
            pltpu.VMEM((ROWS, 128), F32),
            pltpu.VMEM((N, 8, ROWS), F32),
            dma((6,)),
            dma((2, 4, GATHER)), dma((2, 4, GATHER)),
            dma((2, 4, GATHER)), dma((2, 4, GATHER)),
            dma((2, 4, 4)), dma((2, 4, 4)),
            dma, dma,
            dma((N,)), dma((N,)),
            dma((K,)), dma((K,)),
            dma((K, 3)), dma((K, 3)),
            dma((K, 3)), dma((K, 3)),
            dma((K,)), dma((K,)),
            dma((2, 4, ZCH)), dma((2, 4, ZCH)),
            dma((N,)), dma((N,)),
        ],
        compiler_params=pltpu.CompilerParams(
            collective_id=0, has_side_effects=True, vmem_limit_bytes=64 * 2**20
        ),
    )(activations, expert_ids.reshape(1, ROWS), pre_bias, enc_weight, enc_bias, dec_weight)
    return rebuilt, row_error.reshape(ROWS)


def solution(mesh):
    return jax.shard_map(
        local,
        mesh=mesh,
        in_specs=(
            P(("dp", "storage"), "feature"),
            P(("dp", "storage"), None),
            P("dp", "feature"),
            P("dp", "feature", "storage"),
            P("dp", None),
            P("dp", "feature", "storage"),
        ),
        out_specs=(P(("dp", "storage"), "feature"), P(("dp", "storage"))),
        check_vma=False,
    )
```

```python
import functools

import jax
import jax.numpy as jnp
from jax import lax
from jax.experimental import pallas as pl
from jax.experimental.pallas import tpu as pltpu
from jax.sharding import PartitionSpec as P

MESH = pl.DeviceIdType.MESH
D = 4096
N = 8
NX = 4
ROWS = 128
FEAT = 512
BLK = 128
LATS = 512
GATHER = 4
PARTS = ((4,), (3, -3), (2, -2), (1, -1, 0))
K = len(PARTS)
STRIPE = 16
MOST = STRIPE * max(len(p) for p in PARTS)
ZCH = 4
CHUNK = ROWS // ZCH
F32 = jnp.float32
BF16 = jnp.bfloat16


def ring_steps(direction, chunk, chunks):
    far = chunk < chunks // 2 if direction == 0 else chunk >= chunks // 2
    return 4 if far else 3


def kernel(
    act, ids, pre_bias, enc_w, enc_b, dec_w, out, err,
    a_buf, w_buf, w_cat, d_raw, d_buf, pb_raw, eb_raw, ids_raw, meta, ids_all, mask,
    pair_own, pair_out, pair_in, x_own, x_out, x_in, lat, dec, acc_out, acc_in, square, err_all,
    l_sem, a_ss, a_rs, w_ss, w_rs, d_ss, d_rs, m_ss, m_rs, i_ss, i_rs, p_ss, p_rs, x_ss, x_rs, g_ss, g_rs, s_ss, s_rs,
    o_ss, o_rs, e_ss, e_rs,
):
    dp = lax.axis_index("dp")
    storage = lax.axis_index("storage")
    feature = lax.axis_index("feature")
    z = storage % 8
    y = (storage // 8) * 2 + dp
    x = feature // 2
    c = feature % 2

    def at(yy, zz, ff):
        return (yy % 2, (yy // 2) * 8 + zz, ff)

    def z_at(off):
        return at(y, (z + off + N) % N, feature)

    def y_at(off):
        return at((y + off + N) % N, z, feature)

    def f_at(xx, cc):
        return at(y, z, xx * 2 + cc)

    def w_slot(yy):
        return (yy % 2) * 4 + yy // 2

    sibling = f_at(x, 1 - c)
    pending = []

    def send(src, dst, ss, rs, dev):
        cp = pltpu.make_async_remote_copy(
            src_ref=src, dst_ref=dst, send_sem=ss, recv_sem=rs, device_id=dev, device_id_type=MESH
        )
        cp.start()
        pending.append(cp)

    def arrive(dst, ss, rs):
        pltpu.make_async_remote_copy(
            src_ref=dst, dst_ref=dst, send_sem=ss, recv_sem=rs, device_id=sibling, device_id_type=MESH
        ).wait_recv()

    barrier = pltpu.get_barrier_semaphore()
    greet = [z_at(k) for k in range(1, N)] + [y_at(1), y_at(-1)]
    greet += [at(y, z, (feature + k) % 8) for k in range(1, 8)]
    for dev in greet:
        pl.semaphore_signal(barrier, inc=1, device_id=dev, device_id_type=MESH)

    loads = [
        pltpu.make_async_copy(src, dst, l_sem.at[j])
        for j, (src, dst) in enumerate(
            (
                (dec_w.at[0], d_raw),
                (act, a_buf.at[z]),
                (enc_w.at[0], w_buf.at[w_slot(y)]),
                (ids, ids_raw),
                (pre_bias, pb_raw),
                (enc_b, eb_raw),
            )
        )
    ]
    for cp in loads:
        cp.start()
    pl.semaphore_wait(barrier, len(greet))

    def ring_piece(buf, slot_of, coord, chunks, direction, step, chunk):
        sign = 1 if direction == 0 else -1
        block = slot_of((coord - step * sign + N) % N)
        size = buf.shape[1] // chunks
        return buf.at[block, pl.ds(chunk * size, size)]

    def ring_send(buf, first, slot_of, coord, chunks, to, ss, rs, direction, step, chunk):
        ref = ring_piece(buf, slot_of, coord, chunks, direction, step, chunk)
        size = buf.shape[1] // chunks
        src = first.at[pl.ds(chunk * size, size)] if step == 0 else ref
        sign = 1 if direction == 0 else -1
        send(src, ref, ss.at[direction, step, chunk], rs.at[direction, step, chunk], to(sign))

    def ring_arrive(buf, slot_of, coord, chunks, ss, rs, direction, step, chunk):
        ref = ring_piece(buf, slot_of, coord, chunks, direction, step + 1, chunk)
        arrive(ref, ss.at[direction, step, chunk], rs.at[direction, step, chunk])

    a_ring = (a_buf, act, lambda b: b, z, GATHER, z_at, a_ss, a_rs)
    w_ring = (w_buf, enc_w.at[0], w_slot, y, GATHER, y_at, w_ss, w_rs)
    def gather_step(rings, step):
        for chunk in range(GATHER):
            for buf, first, slot_of, coord, chunks, to, ss, rs in rings:
                for direction in range(2):
                    steps = ring_steps(direction, chunk, chunks)
                    if 1 <= step <= steps:
                        ring_arrive(buf, slot_of, coord, chunks, ss, rs, direction, step - 1, chunk)
                    if step < steps:
                        ring_send(buf, first, slot_of, coord, chunks, to, ss, rs, direction, step, chunk)

    def spread(yy):
        lanes = pl.ds(pl.multiple_of((yy // 2) * BLK, BLK), BLK)
        w_cat[yy % 2, :, lanes] = w_buf[w_slot(yy)]

    def d_piece(direction, hop, i):
        piece = (i + 2 * direction) % 4
        block = w_slot((y - hop * (1 - 2 * direction) + N) % N)
        return d_buf.at[block, pl.ds(piece * (BLK // 4), BLK // 4)]

    def d_send(hop, i):
        for direction in range(2):
            ref = d_piece(direction, hop, i)
            send(ref, ref, d_ss.at[direction, hop, i], d_rs.at[direction, hop, i], y_at(1 - 2 * direction))

    def d_arrive(hop, i):
        for direction in range(2):
            arrive(d_piece(direction, hop + 1, i), d_ss.at[direction, hop, i], d_rs.at[direction, hop, i])

    def d_pass(hop, i):
        d_arrive(hop - 1, i)
        d_send(hop, i)

    gather_step((w_ring, a_ring), 0)
    for cp in loads:
        cp.wait()
    d_buf[w_slot(y)] = d_raw[...].astype(F32).T.astype(BF16)
    meta[dp, 0:1, :] = pb_raw[...]
    for q in range(4):
        meta[dp, 1:2, q * BLK:(q + 1) * BLK] = eb_raw[0:1, pl.ds(pl.multiple_of((q * 8 + z) * BLK, BLK), BLK)]
    ids_all[z] = jnp.broadcast_to(ids_raw[...], (8, ROWS))
    send(meta.at[dp], meta.at[dp], m_ss, m_rs, at(y + 1 - 2 * dp, z, feature))
    for k in range(1, N):
        send(ids_all.at[z], ids_all.at[z], i_ss.at[k], i_rs.at[k], z_at(k))
    d_send(0, 0)

    def mask_of(b):
        mask[b] = jnp.broadcast_to(ids_all[b, 0:1, :].astype(F32), (ROWS, ROWS)).T

    mask_of(z)
    spread(y)
    gather_step((w_ring, a_ring), 1)
    d_send(0, 1)
    for k in range(1, N):
        src = (z - k + N) % N
        arrive(ids_all.at[src], i_ss.at[k], i_rs.at[k])
        mask_of(src)
    arrive(meta.at[1 - dp], m_ss, m_rs)
    gather_step((w_ring, a_ring), 2)
    d_send(0, 2)
    d_send(0, 3)
    spread((y + 1) % N)
    spread((y + 7) % N)
    gather_step((w_ring, a_ring), 3)
    spread((y + 2) % N)
    spread((y + 6) % N)
    for i in range(4):
        d_pass(1, i)
    spread((y + 3) % N)
    spread((y + 5) % N)
    gather_step((w_ring, a_ring), 4)
    spread((y + 4) % N)

    def wide(tile):
        return jnp.concatenate([tile] * 4, axis=1) > 0.5

    def stripe(f):
        return pl.ds(pl.multiple_of(f * STRIPE, STRIPE), STRIPE)

    offsets = (2, 1, 3, 0)

    def blocks_of(k):
        return [(z + t + N) % N for t in PARTS[k]]

    def encode(k):
        left, right = [], []
        for f in [2 * ((x + o) % NX) + 1 - c for o in offsets] + [2 * ((x + o) % NX) + c for o in offsets]:
            for b in blocks_of(k):
                second = wide(mask[b, stripe(f), :])
                rows = a_buf[b, stripe(f), :].astype(F32)
                left.append(jnp.where(second, 0.0, rows - meta[0, 0:1, :]).astype(BF16))
                right.append(jnp.where(second, rows - meta[1, 0:1, :], 0.0).astype(BF16))
        sums = jnp.dot(jnp.concatenate(left, 0), w_cat[0], preferred_element_type=F32) + jnp.dot(
            jnp.concatenate(right, 0), w_cat[1], preferred_element_type=F32
        )
        half = NX * STRIPE * len(PARTS[k])
        pair_out[k, :half] = sums[:half].astype(BF16)
        send(pair_out.at[k, pl.ds(0, half)], pair_in.at[k, pl.ds(0, half)], p_ss.at[k], p_rs.at[k], sibling)
        pair_own[k, :half] = sums[half:]

    def pair_sum(k):
        each = STRIPE * len(PARTS[k])
        got = pair_in.at[k, pl.ds(0, NX * each)]
        arrive(got, p_ss.at[k], p_rs.at[k])
        total = pair_own[k, :NX * each] + got[...].astype(F32)
        x_own[k, :each] = total[3 * each:]
        for j in range(3):
            x_out[k, j, :each] = total[j * each:(j + 1) * each].astype(BF16)
            send(
                x_out.at[k, j, pl.ds(0, each)], x_in.at[k, j, pl.ds(0, each)], x_ss.at[k, j], x_rs.at[k, j],
                f_at((x + offsets[j]) % NX, c),
            )

    def lat_of(k, xx):
        each = STRIPE * len(PARTS[k])
        return lat.at[k, c, pl.ds(pl.multiple_of(xx * each, STRIPE), each)]

    def activate(k):
        each = STRIPE * len(PARTS[k])
        pre = x_own[k, :each]
        for j in range(3):
            arrive(x_in.at[k, j, pl.ds(0, each)], x_ss.at[k, j], x_rs.at[k, j])
            pre = pre + x_in[k, j, :each].astype(F32)
        second = jnp.concatenate([wide(mask[b, stripe(feature), :]) for b in blocks_of(k)], 0)
        pre += jnp.where(second, meta[1, 1:2, :], meta[0, 1:2, :])
        mine = lat_of(k, x)
        mine[...] = jnp.maximum(pre, 0.0).astype(BF16)
        for j in range(3):
            send(mine, mine, g_ss.at[k, j], g_rs.at[k, j], f_at((x + offsets[j]) % NX, c))

    def share(k):
        for j in (1, 2, 0):
            arrive(lat_of(k, (x - offsets[j] + NX) % NX), g_ss.at[k, j], g_rs.at[k, j])
        whole = lat.at[k, c, pl.ds(0, NX * STRIPE * len(PARTS[k]))]
        send(whole, whole, s_ss.at[k], s_rs.at[k], sibling)

    def decode(k):
        each = STRIPE * len(PARTS[k])
        arrive(lat.at[k, 1 - c, pl.ds(0, NX * each)], s_ss.at[k], s_rs.at[k])
        left, right = [], []
        for i, b in enumerate(blocks_of(k)):
            second = wide(mask[b])
            starts = [(f % 2, (f // 2) * each + i * STRIPE) for f in range(8)]
            value = jnp.concatenate([lat[k, core, start:start + STRIPE, :] for core, start in starts], 0).astype(F32)
            left.append(jnp.where(second, 0.0, value).astype(BF16))
            right.append(jnp.where(second, value, 0.0).astype(BF16))
        rows = jnp.concatenate([jnp.concatenate(left, 0), jnp.concatenate(right, 0)], axis=1)
        sums = jnp.dot(rows, d_buf[...].reshape(N * BLK, FEAT), preferred_element_type=F32)
        first = sum(len(p) for p in PARTS[:k])
        for i in range(len(PARTS[k])):
            dec[first + i] = sums[i * ROWS:(i + 1) * ROWS]

    def hop(direction, step, h, value):
        acc_out[direction, step, h] = value.astype(BF16)
        send(
            acc_out.at[direction, step, h], acc_in.at[direction, step, h],
            o_ss.at[direction, step, h], o_rs.at[direction, step, h], z_at(1 - 2 * direction),
        )

    def landed(direction, step, h):
        arrive(acc_in.at[direction, step, h], o_ss.at[direction, step, h], o_rs.at[direction, step, h])
        return acc_in[direction, step, h].astype(F32)

    def far(direction, h):
        return h // (ZCH // 2) == direction

    def z_start():
        for i in range(ZCH // 2):
            for direction in range(2):
                h = direction * (ZCH // 2) + i
                hop(direction, 0, h, dec[0, h * CHUNK:(h + 1) * CHUNK])

    def z_step(step):
        for i in range(ZCH):
            for direction in range(2):
                h = (i + (1 - direction) * (ZCH // 2)) % ZCH
                value = dec[2 * step - 1 + direction, h * CHUNK:(h + 1) * CHUNK]
                if step > 1 or far(direction, h):
                    value = value + landed(direction, step - 1, h)
                hop(direction, step, h, value)

    def finish(h):
        span = slice(h * CHUNK, (h + 1) * CHUNK)
        total = dec[7, span] + (landed(0, 3, h) + landed(1, 3, h))
        total += jnp.where(wide(mask[z, span, :]), meta[1, 0:1, :], meta[0, 0:1, :])
        rebuilt = total.astype(BF16)
        out[span, :] = rebuilt
        diff = rebuilt.astype(F32) - a_buf[z, span, :].astype(F32)
        sq = diff * diff
        square[span, :] = sq[:, 0:128] + sq[:, 128:256] + sq[:, 256:384] + sq[:, 384:512]

    def settle(count):
        for cp in pending[:count]:
            cp.wait_send()
        del pending[:count]

    gathered = len(pending)
    encode(0)
    encode(1)
    pair_sum(0)
    d_pass(2, 0)
    encode(2)
    pair_sum(1)
    d_pass(2, 1)
    encode(3)
    pair_sum(2)
    d_pass(2, 2)
    d_pass(2, 3)
    settle(gathered // 2)
    activate(0)
    d_pass(3, 0)
    activate(1)
    d_pass(3, 1)
    pair_sum(3)
    activate(2)
    share(0)
    settle(gathered - gathered // 2)
    d_arrive(2, 2)
    d_arrive(2, 3)
    d_arrive(3, 0)
    d_arrive(3, 1)
    decode(0)
    z_start()
    share(1)
    decode(1)
    activate(3)
    z_step(1)
    share(2)
    decode(2)
    z_step(2)
    share(3)
    decode(3)
    settle(len(pending) - 6 * ZCH)
    z_step(3)
    settle(len(pending) - 2 * ZCH)
    for h in (0, 2, 1, 3):
        finish(h)

    mine = jnp.sum(square[...].T, axis=0, keepdims=True)
    err_all[0] = jnp.broadcast_to(mine, (8, ROWS))
    for k in range(1, 8):
        send(err_all.at[0], err_all.at[k], e_ss.at[k], e_rs.at[k], at(y, z, (feature + k) % 8))
    total = mine
    for k in range(1, 8):
        arrive(err_all.at[k], e_ss.at[k], e_rs.at[k])
        total += err_all[k, 0:1, :]
    err[...] = total * (1.0 / D)
    settle(len(pending))


def local(activations, expert_ids, pre_bias, enc_weight, enc_bias, dec_weight):
    vmem = pl.BlockSpec(memory_space=pltpu.VMEM)
    dma = pltpu.SemaphoreType.DMA
    rebuilt, row_error = pl.pallas_call(
        kernel,
        out_shape=(
            jax.ShapeDtypeStruct((ROWS, FEAT), BF16),
            jax.ShapeDtypeStruct((1, ROWS), F32),
        ),
        in_specs=[pl.BlockSpec(memory_space=pltpu.HBM)] * 6,
        out_specs=(vmem, vmem),
        scratch_shapes=[
            pltpu.VMEM((N, ROWS, FEAT), BF16),
            pltpu.VMEM((N, FEAT, BLK), BF16),
            pltpu.VMEM((2, FEAT, LATS), BF16),
            pltpu.VMEM((FEAT, BLK), BF16),
            pltpu.VMEM((N, BLK, FEAT), BF16),
            pltpu.VMEM((1, FEAT), F32),
            pltpu.VMEM((1, D), F32),
            pltpu.VMEM((1, ROWS), jnp.int32),
            pltpu.VMEM((2, 8, FEAT), F32),
            pltpu.VMEM((N, 8, ROWS), jnp.int32),
            pltpu.VMEM((N, ROWS, ROWS), F32),
            pltpu.VMEM((K, NX * MOST, LATS), F32),
            pltpu.VMEM((K, NX * MOST, LATS), BF16),
            pltpu.VMEM((K, NX * MOST, LATS), BF16),
            pltpu.VMEM((K, MOST, LATS), F32),
            pltpu.VMEM((K, 3, MOST, LATS), BF16),
            pltpu.VMEM((K, 3, MOST, LATS), BF16),
            pltpu.VMEM((K, 2, NX * MOST, LATS), BF16),
            pltpu.VMEM((N, ROWS, FEAT), F32),
            pltpu.VMEM((2, 4, ZCH, CHUNK, FEAT), BF16),
            pltpu.VMEM((2, 4, ZCH, CHUNK, FEAT), BF16),
            pltpu.VMEM((ROWS, 128), F32),
            pltpu.VMEM((N, 8, ROWS), F32),
            dma((6,)),
            dma((2, 4, GATHER)), dma((2, 4, GATHER)),
            dma((2, 4, GATHER)), dma((2, 4, GATHER)),
            dma((2, 4, 4)), dma((2, 4, 4)),
            dma, dma,
            dma((N,)), dma((N,)),
            dma((K,)), dma((K,)),
            dma((K, 3)), dma((K, 3)),
            dma((K, 3)), dma((K, 3)),
            dma((K,)), dma((K,)),
            dma((2, 4, ZCH)), dma((2, 4, ZCH)),
            dma((N,)), dma((N,)),
        ],
        compiler_params=pltpu.CompilerParams(
            collective_id=0, has_side_effects=True, vmem_limit_bytes=64 * 2**20
        ),
    )(activations, expert_ids.reshape(1, ROWS), pre_bias, enc_weight, enc_bias, dec_weight)
    return rebuilt, row_error.reshape(ROWS)


def solution(mesh):
    return jax.shard_map(
        local,
        mesh=mesh,
        in_specs=(
            P(("dp", "storage"), "feature"),
            P(("dp", "storage"), None),
            P("dp", "feature"),
            P("dp", "feature", "storage"),
            P("dp", None),
            P("dp", "feature", "storage"),
        ),
        out_specs=(P(("dp", "storage"), "feature"), P(("dp", "storage"))),
        check_vma=False,
    )
```

```python
import functools

import jax
import jax.numpy as jnp
from jax import lax
from jax.experimental import pallas as pl
from jax.experimental.pallas import tpu as pltpu
from jax.sharding import PartitionSpec as P

MESH = pl.DeviceIdType.MESH
D = 4096
N = 8
NX = 4
ROWS = 128
FEAT = 512
BLK = 128
LATS = 512
GATHER = 4
PARTS = ((4,), (3, -3), (2, -2), (1, -1, 0))
K = len(PARTS)
STRIPE = 16
MOST = STRIPE * max(len(p) for p in PARTS)
ZCH = 4
CHUNK = ROWS // ZCH
F32 = jnp.float32
BF16 = jnp.bfloat16


def ring_steps(direction, chunk, chunks):
    far = chunk < chunks // 2 if direction == 0 else chunk >= chunks // 2
    return 4 if far else 3


def kernel(
    act, ids, pre_bias, enc_w, enc_b, dec_w, out, err,
    a_buf, w_buf, w_cat, d_raw, d_buf, pb_raw, eb_raw, ids_raw, meta, ids_all, mask,
    pair_own, pair_out, pair_in, x_own, x_out, x_in, lat, dec, acc_out, acc_in, square, err_all,
    l_sem, a_ss, a_rs, w_ss, w_rs, d_ss, d_rs, m_ss, m_rs, i_ss, i_rs, p_ss, p_rs, x_ss, x_rs, g_ss, g_rs, s_ss, s_rs,
    o_ss, o_rs, e_ss, e_rs,
):
    dp = lax.axis_index("dp")
    storage = lax.axis_index("storage")
    feature = lax.axis_index("feature")
    z = storage % 8
    y = (storage // 8) * 2 + dp
    x = feature // 2
    c = feature % 2

    def at(yy, zz, ff):
        return (yy % 2, (yy // 2) * 8 + zz, ff)

    def z_at(off):
        return at(y, (z + off + N) % N, feature)

    def y_at(off):
        return at((y + off + N) % N, z, feature)

    def f_at(xx, cc):
        return at(y, z, xx * 2 + cc)

    def w_slot(yy):
        return (yy % 2) * 4 + yy // 2

    sibling = f_at(x, 1 - c)
    pending = []

    def send(src, dst, ss, rs, dev):
        cp = pltpu.make_async_remote_copy(
            src_ref=src, dst_ref=dst, send_sem=ss, recv_sem=rs, device_id=dev, device_id_type=MESH
        )
        cp.start()
        pending.append(cp)

    def arrive(dst, ss, rs):
        pltpu.make_async_remote_copy(
            src_ref=dst, dst_ref=dst, send_sem=ss, recv_sem=rs, device_id=sibling, device_id_type=MESH
        ).wait_recv()

    barrier = pltpu.get_barrier_semaphore()
    greet = [y_at(1), y_at(-1), z_at(1), z_at(-1)] + [z_at(k) for k in range(2, N - 1)]
    greet += [at(y, z, (feature + k) % 8) for k in range(1, 8)]
    for dev in greet:
        pl.semaphore_signal(barrier, inc=1, device_id=dev, device_id_type=MESH)

    loads = [
        pltpu.make_async_copy(src, dst, l_sem.at[j])
        for j, (src, dst) in enumerate(
            (
                (dec_w.at[0], d_raw),
                (act, a_buf.at[z]),
                (enc_w.at[0], w_buf.at[w_slot(y)]),
                (ids, ids_raw),
                (pre_bias, pb_raw),
                (enc_b, eb_raw),
            )
        )
    ]
    pl.semaphore_wait(barrier, len(greet))

    def ring_piece(buf, slot_of, coord, chunks, direction, step, chunk):
        sign = 1 if direction == 0 else -1
        block = slot_of((coord - step * sign + N) % N)
        size = buf.shape[1] // chunks
        return buf.at[block, pl.ds(chunk * size, size)]

    def ring_send(buf, first, slot_of, coord, chunks, to, ss, rs, direction, step, chunk):
        ref = ring_piece(buf, slot_of, coord, chunks, direction, step, chunk)
        size = buf.shape[1] // chunks
        src = first.at[pl.ds(chunk * size, size)] if step == 0 else ref
        sign = 1 if direction == 0 else -1
        send(src, ref, ss.at[direction, step, chunk], rs.at[direction, step, chunk], to(sign))

    def ring_arrive(buf, slot_of, coord, chunks, ss, rs, direction, step, chunk):
        ref = ring_piece(buf, slot_of, coord, chunks, direction, step + 1, chunk)
        arrive(ref, ss.at[direction, step, chunk], rs.at[direction, step, chunk])

    a_ring = (a_buf, act, lambda b: b, z, GATHER, z_at, a_ss, a_rs)
    w_ring = (w_buf, enc_w.at[0], w_slot, y, GATHER, y_at, w_ss, w_rs)
    def gather_step(rings, step):
        for chunk in range(GATHER):
            for buf, first, slot_of, coord, chunks, to, ss, rs in rings:
                for direction in range(2):
                    steps = ring_steps(direction, chunk, chunks)
                    if 1 <= step <= steps:
                        ring_arrive(buf, slot_of, coord, chunks, ss, rs, direction, step - 1, chunk)
                    if step < steps:
                        ring_send(buf, first, slot_of, coord, chunks, to, ss, rs, direction, step, chunk)

    def spread(yy):
        lanes = pl.ds(pl.multiple_of((yy // 2) * BLK, BLK), BLK)
        w_cat[yy % 2, :, lanes] = w_buf[w_slot(yy)]

    def d_piece(direction, hop, i):
        piece = (i + 2 * direction) % 4
        block = w_slot((y - hop * (1 - 2 * direction) + N) % N)
        return d_buf.at[block, pl.ds(piece * (BLK // 4), BLK // 4)]

    def d_send(hop, i):
        for direction in range(2):
            ref = d_piece(direction, hop, i)
            send(ref, ref, d_ss.at[direction, hop, i], d_rs.at[direction, hop, i], y_at(1 - 2 * direction))

    def d_arrive(hop, i):
        for direction in range(2):
            arrive(d_piece(direction, hop + 1, i), d_ss.at[direction, hop, i], d_rs.at[direction, hop, i])

    def d_pass(hop, i):
        d_arrive(hop - 1, i)
        d_send(hop, i)

    gather_step((w_ring, a_ring), 0)
    for cp in loads:
        cp.start()
    for cp in loads:
        cp.wait()
    d_buf[w_slot(y)] = d_raw[...].astype(F32).T.astype(BF16)
    meta[dp, 0:1, :] = pb_raw[...]
    for q in range(4):
        meta[dp, 1:2, q * BLK:(q + 1) * BLK] = eb_raw[0:1, pl.ds(pl.multiple_of((q * 8 + z) * BLK, BLK), BLK)]
    ids_all[z] = jnp.broadcast_to(ids_raw[...], (8, ROWS))
    send(meta.at[dp], meta.at[dp], m_ss, m_rs, at(y + 1 - 2 * dp, z, feature))
    for k in range(1, N):
        send(ids_all.at[z], ids_all.at[z], i_ss.at[k], i_rs.at[k], z_at(k))
    d_send(0, 0)

    def mask_of(b):
        mask[b] = jnp.broadcast_to(ids_all[b, 0:1, :].astype(F32), (ROWS, ROWS)).T

    spread(y)
    gather_step((w_ring, a_ring), 1)
    d_send(0, 1)
    for k in range(1, N):
        arrive(ids_all.at[(z - k + N) % N], i_ss.at[k], i_rs.at[k])
    arrive(meta.at[1 - dp], m_ss, m_rs)
    mask_of(z)
    mask_of((z + 4) % N)
    gather_step((w_ring, a_ring), 2)
    d_send(0, 2)
    d_send(0, 3)
    for k in (1, 2, 3):
        mask_of((z + k) % N)
    spread((y + 1) % N)
    spread((y + 7) % N)
    gather_step((w_ring, a_ring), 3)
    spread((y + 2) % N)
    spread((y + 6) % N)
    for i in range(4):
        d_pass(1, i)
    for k in (5, 6, 7):
        mask_of((z + k) % N)
    spread((y + 3) % N)
    spread((y + 5) % N)
    gather_step((w_ring, a_ring), 4)
    spread((y + 4) % N)

    def wide(tile):
        return jnp.concatenate([tile] * 4, axis=1) > 0.5

    def stripe(f):
        return pl.ds(pl.multiple_of(f * STRIPE, STRIPE), STRIPE)

    offsets = (2, 1, 3, 0)

    def blocks_of(k):
        return [(z + t + N) % N for t in PARTS[k]]

    def encode(k):
        left, right = [], []
        for f in [2 * ((x + o) % NX) + 1 - c for o in offsets] + [2 * ((x + o) % NX) + c for o in offsets]:
            for b in blocks_of(k):
                second = wide(mask[b, stripe(f), :])
                rows = a_buf[b, stripe(f), :].astype(F32)
                left.append(jnp.where(second, 0.0, rows - meta[0, 0:1, :]).astype(BF16))
                right.append(jnp.where(second, rows - meta[1, 0:1, :], 0.0).astype(BF16))
        sums = jnp.dot(jnp.concatenate(left, 0), w_cat[0], preferred_element_type=F32) + jnp.dot(
            jnp.concatenate(right, 0), w_cat[1], preferred_element_type=F32
        )
        half = NX * STRIPE * len(PARTS[k])
        pair_out[k, :half] = sums[:half].astype(BF16)
        send(pair_out.at[k, pl.ds(0, half)], pair_in.at[k, pl.ds(0, half)], p_ss.at[k], p_rs.at[k], sibling)
        pair_own[k, :half] = sums[half:]

    def pair_sum(k):
        each = STRIPE * len(PARTS[k])
        got = pair_in.at[k, pl.ds(0, NX * each)]
        arrive(got, p_ss.at[k], p_rs.at[k])
        total = pair_own[k, :NX * each] + got[...].astype(F32)
        x_own[k, :each] = total[3 * each:]
        for j in range(3):
            x_out[k, j, :each] = total[j * each:(j + 1) * each].astype(BF16)
            send(
                x_out.at[k, j, pl.ds(0, each)], x_in.at[k, j, pl.ds(0, each)], x_ss.at[k, j], x_rs.at[k, j],
                f_at((x + offsets[j]) % NX, c),
            )

    def lat_of(k, xx):
        each = STRIPE * len(PARTS[k])
        return lat.at[k, c, pl.ds(pl.multiple_of(xx * each, STRIPE), each)]

    def activate(k):
        each = STRIPE * len(PARTS[k])
        pre = x_own[k, :each]
        for j in range(3):
            arrive(x_in.at[k, j, pl.ds(0, each)], x_ss.at[k, j], x_rs.at[k, j])
            pre = pre + x_in[k, j, :each].astype(F32)
        second = jnp.concatenate([wide(mask[b, stripe(feature), :]) for b in blocks_of(k)], 0)
        pre += jnp.where(second, meta[1, 1:2, :], meta[0, 1:2, :])
        mine = lat_of(k, x)
        mine[...] = jnp.maximum(pre, 0.0).astype(BF16)
        for j in range(3):
            send(mine, mine, g_ss.at[k, j], g_rs.at[k, j], f_at((x + offsets[j]) % NX, c))

    def share(k):
        for j in (1, 2, 0):
            arrive(lat_of(k, (x - offsets[j] + NX) % NX), g_ss.at[k, j], g_rs.at[k, j])
        whole = lat.at[k, c, pl.ds(0, NX * STRIPE * len(PARTS[k]))]
        send(whole, whole, s_ss.at[k], s_rs.at[k], sibling)

    def decode(k):
        each = STRIPE * len(PARTS[k])
        arrive(lat.at[k, 1 - c, pl.ds(0, NX * each)], s_ss.at[k], s_rs.at[k])
        left, right = [], []
        for i, b in enumerate(blocks_of(k)):
            second = wide(mask[b])
            starts = [(f % 2, (f // 2) * each + i * STRIPE) for f in range(8)]
            value = jnp.concatenate([lat[k, core, start:start + STRIPE, :] for core, start in starts], 0).astype(F32)
            left.append(jnp.where(second, 0.0, value).astype(BF16))
            right.append(jnp.where(second, value, 0.0).astype(BF16))
        rows = jnp.concatenate([jnp.concatenate(left, 0), jnp.concatenate(right, 0)], axis=1)
        sums = jnp.dot(rows, d_buf[...].reshape(N * BLK, FEAT), preferred_element_type=F32)
        first = sum(len(p) for p in PARTS[:k])
        for i in range(len(PARTS[k])):
            dec[first + i] = sums[i * ROWS:(i + 1) * ROWS]

    def hop(direction, step, h, value):
        acc_out[direction, step, h] = value.astype(BF16)
        send(
            acc_out.at[direction, step, h], acc_in.at[direction, step, h],
            o_ss.at[direction, step, h], o_rs.at[direction, step, h], z_at(1 - 2 * direction),
        )

    def landed(direction, step, h):
        arrive(acc_in.at[direction, step, h], o_ss.at[direction, step, h], o_rs.at[direction, step, h])
        return acc_in[direction, step, h].astype(F32)

    def far(direction, h):
        return h // (ZCH // 2) == direction

    def z_start():
        for i in range(ZCH // 2):
            for direction in range(2):
                h = direction * (ZCH // 2) + i
                hop(direction, 0, h, dec[0, h * CHUNK:(h + 1) * CHUNK])

    def z_step(step):
        for i in range(ZCH):
            for direction in range(2):
                h = (i + (1 - direction) * (ZCH // 2)) % ZCH
                value = dec[2 * step - 1 + direction, h * CHUNK:(h + 1) * CHUNK]
                if step > 1 or far(direction, h):
                    value = value + landed(direction, step - 1, h)
                hop(direction, step, h, value)

    def finish(h):
        span = slice(h * CHUNK, (h + 1) * CHUNK)
        total = dec[7, span] + (landed(0, 3, h) + landed(1, 3, h))
        total += jnp.where(wide(mask[z, span, :]), meta[1, 0:1, :], meta[0, 0:1, :])
        rebuilt = total.astype(BF16)
        out[span, :] = rebuilt
        diff = rebuilt.astype(F32) - a_buf[z, span, :].astype(F32)
        sq = diff * diff
        square[span, :] = sq[:, 0:128] + sq[:, 128:256] + sq[:, 256:384] + sq[:, 384:512]

    def settle(count):
        for cp in pending[:count]:
            cp.wait_send()
        del pending[:count]

    gathered = len(pending)
    encode(0)
    encode(1)
    pair_sum(0)
    d_pass(2, 0)
    encode(2)
    pair_sum(1)
    d_pass(2, 1)
    encode(3)
    pair_sum(2)
    d_pass(2, 2)
    d_pass(2, 3)
    settle(gathered // 2)
    activate(0)
    d_pass(3, 0)
    activate(1)
    d_pass(3, 1)
    pair_sum(3)
    activate(2)
    share(0)
    settle(gathered - gathered // 2)
    d_arrive(2, 2)
    d_arrive(2, 3)
    d_arrive(3, 0)
    d_arrive(3, 1)
    decode(0)
    z_start()
    share(1)
    decode(1)
    z_step(1)
    activate(3)
    share(2)
    decode(2)
    z_step(2)
    share(3)
    decode(3)
    settle(len(pending) - 6 * ZCH)
    z_step(3)
    settle(len(pending) - 2 * ZCH)
    for h in (0, 2, 1, 3):
        finish(h)

    mine = jnp.sum(square[...].T, axis=0, keepdims=True)
    err_all[0] = jnp.broadcast_to(mine, (8, ROWS))
    for k in range(1, 8):
        send(err_all.at[0], err_all.at[k], e_ss.at[k], e_rs.at[k], at(y, z, (feature + k) % 8))
    total = mine
    for k in range(1, 8):
        arrive(err_all.at[k], e_ss.at[k], e_rs.at[k])
        total += err_all[k, 0:1, :]
    err[...] = total * (1.0 / D)
    settle(len(pending))


def local(activations, expert_ids, pre_bias, enc_weight, enc_bias, dec_weight):
    vmem = pl.BlockSpec(memory_space=pltpu.VMEM)
    dma = pltpu.SemaphoreType.DMA
    rebuilt, row_error = pl.pallas_call(
        kernel,
        out_shape=(
            jax.ShapeDtypeStruct((ROWS, FEAT), BF16),
            jax.ShapeDtypeStruct((1, ROWS), F32),
        ),
        in_specs=[pl.BlockSpec(memory_space=pltpu.HBM)] * 6,
        out_specs=(vmem, vmem),
        scratch_shapes=[
            pltpu.VMEM((N, ROWS, FEAT), BF16),
            pltpu.VMEM((N, FEAT, BLK), BF16),
            pltpu.VMEM((2, FEAT, LATS), BF16),
            pltpu.VMEM((FEAT, BLK), BF16),
            pltpu.VMEM((N, BLK, FEAT), BF16),
            pltpu.VMEM((1, FEAT), F32),
            pltpu.VMEM((1, D), F32),
            pltpu.VMEM((1, ROWS), jnp.int32),
            pltpu.VMEM((2, 8, FEAT), F32),
            pltpu.VMEM((N, 8, ROWS), jnp.int32),
            pltpu.VMEM((N, ROWS, ROWS), F32),
            pltpu.VMEM((K, NX * MOST, LATS), F32),
            pltpu.VMEM((K, NX * MOST, LATS), BF16),
            pltpu.VMEM((K, NX * MOST, LATS), BF16),
            pltpu.VMEM((K, MOST, LATS), F32),
            pltpu.VMEM((K, 3, MOST, LATS), BF16),
            pltpu.VMEM((K, 3, MOST, LATS), BF16),
            pltpu.VMEM((K, 2, NX * MOST, LATS), BF16),
            pltpu.VMEM((N, ROWS, FEAT), F32),
            pltpu.VMEM((2, 4, ZCH, CHUNK, FEAT), BF16),
            pltpu.VMEM((2, 4, ZCH, CHUNK, FEAT), BF16),
            pltpu.VMEM((ROWS, 128), F32),
            pltpu.VMEM((N, 8, ROWS), F32),
            dma((6,)),
            dma((2, 4, GATHER)), dma((2, 4, GATHER)),
            dma((2, 4, GATHER)), dma((2, 4, GATHER)),
            dma((2, 4, 4)), dma((2, 4, 4)),
            dma, dma,
            dma((N,)), dma((N,)),
            dma((K,)), dma((K,)),
            dma((K, 3)), dma((K, 3)),
            dma((K, 3)), dma((K, 3)),
            dma((K,)), dma((K,)),
            dma((2, 4, ZCH)), dma((2, 4, ZCH)),
            dma((N,)), dma((N,)),
        ],
        compiler_params=pltpu.CompilerParams(
            collective_id=0, has_side_effects=True, vmem_limit_bytes=64 * 2**20
        ),
    )(activations, expert_ids.reshape(1, ROWS), pre_bias, enc_weight, enc_bias, dec_weight)
    return rebuilt, row_error.reshape(ROWS)


def solution(mesh):
    return jax.shard_map(
        local,
        mesh=mesh,
        in_specs=(
            P(("dp", "storage"), "feature"),
            P(("dp", "storage"), None),
            P("dp", "feature"),
            P("dp", "feature", "storage"),
            P("dp", None),
            P("dp", "feature", "storage"),
        ),
        out_specs=(P(("dp", "storage"), "feature"), P(("dp", "storage"))),
        check_vma=False,
    )
```

```python
import functools

import jax
import jax.numpy as jnp
from jax import lax
from jax.experimental import pallas as pl
from jax.experimental.pallas import tpu as pltpu
from jax.sharding import PartitionSpec as P

MESH = pl.DeviceIdType.MESH
D = 4096
N = 8
NX = 4
ROWS = 128
FEAT = 512
BLK = 128
LATS = 512
GATHER = 4
PARTS = ((4,), (3, -3), (2, -2), (1, -1, 0))
K = len(PARTS)
STRIPE = 16
MOST = STRIPE * max(len(p) for p in PARTS)
ZCH = 4
CHUNK = ROWS // ZCH
F32 = jnp.float32
BF16 = jnp.bfloat16


def ring_steps(direction, chunk, chunks):
    far = chunk < chunks // 2 if direction == 0 else chunk >= chunks // 2
    return 4 if far else 3


def kernel(
    act, ids, pre_bias, enc_w, enc_b, dec_w, out, err,
    a_buf, w_buf, w_cat, d_raw, d_buf, pb_raw, eb_raw, ids_raw, meta, ids_all, mask,
    pair_own, pair_out, pair_in, x_own, x_out, x_in, lat, dec, acc_out, acc_in, square, err_all,
    l_sem, a_ss, a_rs, w_ss, w_rs, d_ss, d_rs, m_ss, m_rs, i_ss, i_rs, p_ss, p_rs, x_ss, x_rs, g_ss, g_rs, s_ss, s_rs,
    o_ss, o_rs, e_ss, e_rs,
):
    dp = lax.axis_index("dp")
    storage = lax.axis_index("storage")
    feature = lax.axis_index("feature")
    z = storage % 8
    y = (storage // 8) * 2 + dp
    x = feature // 2
    c = feature % 2

    def at(yy, zz, ff):
        return (yy % 2, (yy // 2) * 8 + zz, ff)

    def z_at(off):
        return at(y, (z + off + N) % N, feature)

    def y_at(off):
        return at((y + off + N) % N, z, feature)

    def f_at(xx, cc):
        return at(y, z, xx * 2 + cc)

    def w_slot(yy):
        return (yy % 2) * 4 + yy // 2

    sibling = f_at(x, 1 - c)
    pending = []

    def send(src, dst, ss, rs, dev):
        cp = pltpu.make_async_remote_copy(
            src_ref=src, dst_ref=dst, send_sem=ss, recv_sem=rs, device_id=dev, device_id_type=MESH
        )
        cp.start()
        pending.append(cp)

    def arrive(dst, ss, rs):
        pltpu.make_async_remote_copy(
            src_ref=dst, dst_ref=dst, send_sem=ss, recv_sem=rs, device_id=sibling, device_id_type=MESH
        ).wait_recv()

    barrier = pltpu.get_barrier_semaphore()
    greet = [y_at(1), y_at(-1), z_at(1), z_at(-1)] + [z_at(k) for k in range(2, N - 1)]
    greet += [at(y, z, (feature + k) % 8) for k in range(1, 8)]
    for dev in greet:
        pl.semaphore_signal(barrier, inc=1, device_id=dev, device_id_type=MESH)

    loads = [
        pltpu.make_async_copy(src, dst, l_sem.at[j])
        for j, (src, dst) in enumerate(
            (
                (dec_w.at[0], d_raw),
                (act, a_buf.at[z]),
                (enc_w.at[0], w_buf.at[w_slot(y)]),
                (ids, ids_raw),
                (pre_bias, pb_raw),
                (enc_b, eb_raw),
            )
        )
    ]
    pl.semaphore_wait(barrier, len(greet))

    def ring_piece(buf, slot_of, coord, chunks, direction, step, chunk):
        sign = 1 if direction == 0 else -1
        block = slot_of((coord - step * sign + N) % N)
        size = buf.shape[1] // chunks
        return buf.at[block, pl.ds(chunk * size, size)]

    def ring_send(buf, first, slot_of, coord, chunks, to, ss, rs, direction, step, chunk):
        ref = ring_piece(buf, slot_of, coord, chunks, direction, step, chunk)
        size = buf.shape[1] // chunks
        src = first.at[pl.ds(chunk * size, size)] if step == 0 else ref
        sign = 1 if direction == 0 else -1
        send(src, ref, ss.at[direction, step, chunk], rs.at[direction, step, chunk], to(sign))

    def ring_arrive(buf, slot_of, coord, chunks, ss, rs, direction, step, chunk):
        ref = ring_piece(buf, slot_of, coord, chunks, direction, step + 1, chunk)
        arrive(ref, ss.at[direction, step, chunk], rs.at[direction, step, chunk])

    a_ring = (a_buf, act, lambda b: b, z, GATHER, z_at, a_ss, a_rs)
    w_ring = (w_buf, enc_w.at[0], w_slot, y, GATHER, y_at, w_ss, w_rs)
    def gather_step(rings, step):
        for chunk in range(GATHER):
            for buf, first, slot_of, coord, chunks, to, ss, rs in rings:
                for direction in range(2):
                    steps = ring_steps(direction, chunk, chunks)
                    if 1 <= step <= steps:
                        ring_arrive(buf, slot_of, coord, chunks, ss, rs, direction, step - 1, chunk)
                    if step < steps:
                        ring_send(buf, first, slot_of, coord, chunks, to, ss, rs, direction, step, chunk)

    def spread(yy):
        lanes = pl.ds(pl.multiple_of((yy // 2) * BLK, BLK), BLK)
        w_cat[yy % 2, :, lanes] = w_buf[w_slot(yy)]

    def d_piece(direction, hop, i):
        piece = (i + 2 * direction) % 4
        block = w_slot((y - hop * (1 - 2 * direction) + N) % N)
        return d_buf.at[block, pl.ds(piece * (BLK // 4), BLK // 4)]

    def d_send(hop, i):
        for direction in range(2):
            ref = d_piece(direction, hop, i)
            send(ref, ref, d_ss.at[direction, hop, i], d_rs.at[direction, hop, i], y_at(1 - 2 * direction))

    def d_arrive(hop, i):
        for direction in range(2):
            arrive(d_piece(direction, hop + 1, i), d_ss.at[direction, hop, i], d_rs.at[direction, hop, i])

    def d_pass(hop, i):
        d_arrive(hop - 1, i)
        d_send(hop, i)

    gather_step((w_ring, a_ring), 0)
    for cp in loads:
        cp.start()
    for cp in loads:
        cp.wait()
    d_buf[w_slot(y)] = d_raw[...].astype(F32).T.astype(BF16)
    meta[dp, 0:1, :] = pb_raw[...]
    for q in range(4):
        meta[dp, 1:2, q * BLK:(q + 1) * BLK] = eb_raw[0:1, pl.ds(pl.multiple_of((q * 8 + z) * BLK, BLK), BLK)]
    ids_all[z] = jnp.broadcast_to(ids_raw[...], (8, ROWS))
    send(meta.at[dp], meta.at[dp], m_ss, m_rs, at(y + 1 - 2 * dp, z, feature))
    for k in range(1, N):
        send(ids_all.at[z], ids_all.at[z], i_ss.at[k], i_rs.at[k], z_at(k))
    d_send(0, 0)

    def mask_of(b):
        mask[b] = jnp.broadcast_to(ids_all[b, 0:1, :].astype(F32), (ROWS, ROWS)).T

    spread(y)
    gather_step((w_ring, a_ring), 1)
    d_send(0, 1)
    for k in range(1, N):
        arrive(ids_all.at[(z - k + N) % N], i_ss.at[k], i_rs.at[k])
    arrive(meta.at[1 - dp], m_ss, m_rs)
    mask_of(z)
    mask_of((z + 4) % N)
    gather_step((w_ring, a_ring), 2)
    d_send(0, 2)
    d_send(0, 3)
    for k in (1, 2, 3):
        mask_of((z + k) % N)
    spread((y + 1) % N)
    spread((y + 7) % N)
    gather_step((w_ring, a_ring), 3)
    spread((y + 2) % N)
    spread((y + 6) % N)
    for i in range(4):
        d_pass(1, i)
    for k in (5, 6, 7):
        mask_of((z + k) % N)
    spread((y + 3) % N)
    spread((y + 5) % N)
    gather_step((w_ring, a_ring), 4)
    spread((y + 4) % N)

    def wide(tile):
        return jnp.concatenate([tile] * 4, axis=1) > 0.5

    def stripe(f):
        return pl.ds(pl.multiple_of(f * STRIPE, STRIPE), STRIPE)

    offsets = (2, 1, 3, 0)

    def blocks_of(k):
        return [(z + t + N) % N for t in PARTS[k]]

    def encode(k):
        left, right = [], []
        for f in [2 * ((x + o) % NX) + 1 - c for o in offsets] + [2 * ((x + o) % NX) + c for o in offsets]:
            for b in blocks_of(k):
                second = wide(mask[b, stripe(f), :])
                rows = a_buf[b, stripe(f), :].astype(F32)
                left.append(jnp.where(second, 0.0, rows - meta[0, 0:1, :]).astype(BF16))
                right.append(jnp.where(second, rows - meta[1, 0:1, :], 0.0).astype(BF16))
        sums = jnp.dot(jnp.concatenate(left, 0), w_cat[0], preferred_element_type=F32) + jnp.dot(
            jnp.concatenate(right, 0), w_cat[1], preferred_element_type=F32
        )
        half = NX * STRIPE * len(PARTS[k])
        pair_out[k, :half] = sums[:half].astype(BF16)
        send(pair_out.at[k, pl.ds(0, half)], pair_in.at[k, pl.ds(0, half)], p_ss.at[k], p_rs.at[k], sibling)
        pair_own[k, :half] = sums[half:]

    def pair_sum(k):
        each = STRIPE * len(PARTS[k])
        got = pair_in.at[k, pl.ds(0, NX * each)]
        arrive(got, p_ss.at[k], p_rs.at[k])
        total = pair_own[k, :NX * each] + got[...].astype(F32)
        x_own[k, :each] = total[3 * each:]
        for j in range(3):
            x_out[k, j, :each] = total[j * each:(j + 1) * each].astype(BF16)
            send(
                x_out.at[k, j, pl.ds(0, each)], x_in.at[k, j, pl.ds(0, each)], x_ss.at[k, j], x_rs.at[k, j],
                f_at((x + offsets[j]) % NX, c),
            )

    def lat_of(k, xx):
        each = STRIPE * len(PARTS[k])
        return lat.at[k, c, pl.ds(pl.multiple_of(xx * each, STRIPE), each)]

    def activate(k):
        each = STRIPE * len(PARTS[k])
        pre = x_own[k, :each]
        for j in range(3):
            arrive(x_in.at[k, j, pl.ds(0, each)], x_ss.at[k, j], x_rs.at[k, j])
            pre = pre + x_in[k, j, :each].astype(F32)
        second = jnp.concatenate([wide(mask[b, stripe(feature), :]) for b in blocks_of(k)], 0)
        pre += jnp.where(second, meta[1, 1:2, :], meta[0, 1:2, :])
        mine = lat_of(k, x)
        mine[...] = jnp.maximum(pre, 0.0).astype(BF16)
        for j in range(3):
            send(mine, mine, g_ss.at[k, j], g_rs.at[k, j], f_at((x + offsets[j]) % NX, c))

    def share(k):
        for j in (1, 2, 0):
            arrive(lat_of(k, (x - offsets[j] + NX) % NX), g_ss.at[k, j], g_rs.at[k, j])
        whole = lat.at[k, c, pl.ds(0, NX * STRIPE * len(PARTS[k]))]
        send(whole, whole, s_ss.at[k], s_rs.at[k], sibling)

    def decode(k):
        each = STRIPE * len(PARTS[k])
        arrive(lat.at[k, 1 - c, pl.ds(0, NX * each)], s_ss.at[k], s_rs.at[k])
        left, right = [], []
        for i, b in enumerate(blocks_of(k)):
            second = wide(mask[b])
            starts = [(f % 2, (f // 2) * each + i * STRIPE) for f in range(8)]
            value = jnp.concatenate([lat[k, core, start:start + STRIPE, :] for core, start in starts], 0).astype(F32)
            left.append(jnp.where(second, 0.0, value).astype(BF16))
            right.append(jnp.where(second, value, 0.0).astype(BF16))
        rows = jnp.concatenate([jnp.concatenate(left, 0), jnp.concatenate(right, 0)], axis=1)
        sums = jnp.dot(rows, d_buf[...].reshape(N * BLK, FEAT), preferred_element_type=F32)
        first = sum(len(p) for p in PARTS[:k])
        for i in range(len(PARTS[k])):
            dec[first + i] = sums[i * ROWS:(i + 1) * ROWS]

    def hop(direction, step, h, value):
        acc_out[direction, step, h] = value.astype(BF16)
        send(
            acc_out.at[direction, step, h], acc_in.at[direction, step, h],
            o_ss.at[direction, step, h], o_rs.at[direction, step, h], z_at(1 - 2 * direction),
        )

    def landed(direction, step, h):
        arrive(acc_in.at[direction, step, h], o_ss.at[direction, step, h], o_rs.at[direction, step, h])
        return acc_in[direction, step, h].astype(F32)

    def far(direction, h):
        return h // (ZCH // 2) == direction

    def z_start():
        for i in range(ZCH // 2):
            for direction in range(2):
                h = direction * (ZCH // 2) + i
                hop(direction, 0, h, dec[0, h * CHUNK:(h + 1) * CHUNK])

    def z_step(step):
        for i in range(ZCH):
            for direction in range(2):
                h = (i + (1 - direction) * (ZCH // 2)) % ZCH
                value = dec[2 * step - 1 + direction, h * CHUNK:(h + 1) * CHUNK]
                if step > 1 or far(direction, h):
                    value = value + landed(direction, step - 1, h)
                hop(direction, step, h, value)

    def finish(h):
        span = slice(h * CHUNK, (h + 1) * CHUNK)
        total = dec[7, span] + (landed(0, 3, h) + landed(1, 3, h))
        total += jnp.where(wide(mask[z, span, :]), meta[1, 0:1, :], meta[0, 0:1, :])
        rebuilt = total.astype(BF16)
        out[span, :] = rebuilt
        diff = rebuilt.astype(F32) - a_buf[z, span, :].astype(F32)
        sq = diff * diff
        square[span, :] = sq[:, 0:128] + sq[:, 128:256] + sq[:, 256:384] + sq[:, 384:512]

    def settle(count):
        for cp in pending[:count]:
            cp.wait_send()
        del pending[:count]

    gathered = len(pending)
    encode(0)
    encode(1)
    pair_sum(0)
    d_pass(2, 0)
    encode(2)
    pair_sum(1)
    d_pass(2, 1)
    encode(3)
    pair_sum(2)
    d_pass(2, 2)
    d_pass(2, 3)
    settle(gathered // 2)
    activate(0)
    d_pass(3, 0)
    activate(1)
    d_pass(3, 1)
    share(0)
    activate(2)
    pair_sum(3)
    settle(gathered - gathered // 2)
    d_arrive(2, 2)
    d_arrive(2, 3)
    d_arrive(3, 0)
    d_arrive(3, 1)
    decode(0)
    z_start()
    share(1)
    decode(1)
    z_step(1)
    activate(3)
    share(2)
    decode(2)
    z_step(2)
    share(3)
    decode(3)
    z_step(3)
    settle(len(pending) - 2 * ZCH)
    for h in (2, 0, 3, 1):
        finish(h)

    mine = jnp.sum(square[...].T, axis=0, keepdims=True)
    err_all[0] = jnp.broadcast_to(mine, (8, ROWS))
    for k in range(1, 8):
        send(err_all.at[0, pl.ds(0, 1)], err_all.at[k, pl.ds(0, 1)], e_ss.at[k], e_rs.at[k], at(y, z, (feature + k) % 8))
    total = mine
    for k in range(1, 8):
        arrive(err_all.at[k, pl.ds(0, 1)], e_ss.at[k], e_rs.at[k])
        total += err_all[k, 0:1, :]
    err[...] = total * (1.0 / D)
    settle(len(pending))


def local(activations, expert_ids, pre_bias, enc_weight, enc_bias, dec_weight):
    vmem = pl.BlockSpec(memory_space=pltpu.VMEM)
    dma = pltpu.SemaphoreType.DMA
    rebuilt, row_error = pl.pallas_call(
        kernel,
        out_shape=(
            jax.ShapeDtypeStruct((ROWS, FEAT), BF16),
            jax.ShapeDtypeStruct((1, ROWS), F32),
        ),
        in_specs=[pl.BlockSpec(memory_space=pltpu.HBM)] * 6,
        out_specs=(vmem, vmem),
        scratch_shapes=[
            pltpu.VMEM((N, ROWS, FEAT), BF16),
            pltpu.VMEM((N, FEAT, BLK), BF16),
            pltpu.VMEM((2, FEAT, LATS), BF16),
            pltpu.VMEM((FEAT, BLK), BF16),
            pltpu.VMEM((N, BLK, FEAT), BF16),
            pltpu.VMEM((1, FEAT), F32),
            pltpu.VMEM((1, D), F32),
            pltpu.VMEM((1, ROWS), jnp.int32),
            pltpu.VMEM((2, 8, FEAT), F32),
            pltpu.VMEM((N, 8, ROWS), jnp.int32),
            pltpu.VMEM((N, ROWS, ROWS), F32),
            pltpu.VMEM((K, NX * MOST, LATS), F32),
            pltpu.VMEM((K, NX * MOST, LATS), BF16),
            pltpu.VMEM((K, NX * MOST, LATS), BF16),
            pltpu.VMEM((K, MOST, LATS), F32),
            pltpu.VMEM((K, 3, MOST, LATS), BF16),
            pltpu.VMEM((K, 3, MOST, LATS), BF16),
            pltpu.VMEM((K, 2, NX * MOST, LATS), BF16),
            pltpu.VMEM((N, ROWS, FEAT), F32),
            pltpu.VMEM((2, 4, ZCH, CHUNK, FEAT), BF16),
            pltpu.VMEM((2, 4, ZCH, CHUNK, FEAT), BF16),
            pltpu.VMEM((ROWS, 128), F32),
            pltpu.VMEM((N, 8, ROWS), F32),
            dma((6,)),
            dma((2, 4, GATHER)), dma((2, 4, GATHER)),
            dma((2, 4, GATHER)), dma((2, 4, GATHER)),
            dma((2, 4, 4)), dma((2, 4, 4)),
            dma, dma,
            dma((N,)), dma((N,)),
            dma((K,)), dma((K,)),
            dma((K, 3)), dma((K, 3)),
            dma((K, 3)), dma((K, 3)),
            dma((K,)), dma((K,)),
            dma((2, 4, ZCH)), dma((2, 4, ZCH)),
            dma((N,)), dma((N,)),
        ],
        compiler_params=pltpu.CompilerParams(
            collective_id=0, has_side_effects=True, vmem_limit_bytes=64 * 2**20
        ),
    )(activations, expert_ids.reshape(1, ROWS), pre_bias, enc_weight, enc_bias, dec_weight)
    return rebuilt, row_error.reshape(ROWS)


def solution(mesh):
    return jax.shard_map(
        local,
        mesh=mesh,
        in_specs=(
            P(("dp", "storage"), "feature"),
            P(("dp", "storage"), None),
            P("dp", "feature"),
            P("dp", "feature", "storage"),
            P("dp", None),
            P("dp", "feature", "storage"),
        ),
        out_specs=(P(("dp", "storage"), "feature"), P(("dp", "storage"))),
        check_vma=False,
    )
```
